32 devices in a mesh: seq: 8 (over z, x), head: 4 (over y, core).
Axes of the slice: x: 2, y: 2, z: 4, core: 2. Of those that a mesh axis runs over, the one named last changes fastest.
Arguments:
- tokens: bfloat16 [4096, 1024], P(('seq', 'head')), may hold values from -6 to 6
- doc_starts: int32 [8], replicated, may hold values from 0 to 4095, as said below
- conv_norm: bfloat16 [1024], P(('seq', 'head')), may hold values from 0.5 to 1.5
- conv_in: bfloat16 [1024, 3072], P(('seq', 'head')), may hold values from -0.1875 to 0.1875
- conv_kernel: bfloat16 [1024, 3], P(('seq', 'head')), may hold values from -3.5 to 3.5
- conv_out: bfloat16 [1024, 1024], P(('seq', 'head')), may hold values from -0.1875 to 0.1875
- ffn1_norm: bfloat16 [1024], P(('seq', 'head')), may hold values from 0.5 to 1.5
- ffn1_gate: bfloat16 [1024, 4608], P(None, ('seq', 'head')), may hold values from -0.1875 to 0.1875
- ffn1_up: bfloat16 [1024, 4608], P(None, ('seq', 'head')), may hold values from -0.1875 to 0.1875
- ffn1_down: bfloat16 [4608, 1024], P(('seq', 'head')), may hold values from -0.09375 to 0.09375
- attn_norm: bfloat16 [1024], P(('seq', 'head')), may hold values from 0.5 to 1.5
- attn_query: bfloat16 [1024, 1024], P(('seq', 'head')), may hold values from -0.1875 to 0.1875
- attn_key: bfloat16 [1024, 512], P(('seq', 'head')), may hold values from -0.1875 to 0.1875
- attn_value: bfloat16 [1024, 512], P(('seq', 'head')), may hold values from -0.1875 to 0.1875
- qk_gains: bfloat16 [2, 64], replicated, may hold values from 0.5 to 1.5
- attn_output: bfloat16 [1024, 1024], P(('seq', 'head')), may hold values from -3 to 3
- ffn2_norm: bfloat16 [1024], P(('seq', 'head')), may hold values from 0.5 to 1.5
- ffn2_gate: bfloat16 [1024, 4608], P(None, ('seq', 'head')), may hold values from -0.1875 to 0.1875
- ffn2_up: bfloat16 [1024, 4608], P(None, ('seq', 'head')), may hold values from -0.1875 to 0.1875
- ffn2_down: bfloat16 [4608, 1024], P(('seq', 'head')), may hold values from -0.09375 to 0.09375
- cotangent: bfloat16 [4096, 1024], P(('seq', 'head')), may hold values from -6 to 6
Outputs:
- output: bfloat16 [4096, 1024], P(('seq', 'head'))
- grad_tokens: float32 [4096, 1024], P(('seq', 'head'))
- grad_conv_norm: float32 [1024], P(('seq', 'head'))
- grad_conv_in: float32 [1024, 3072], P(('seq', 'head'))
- grad_conv_kernel: float32 [1024, 3], P(('seq', 'head'))
- grad_conv_out: float32 [1024, 1024], P(('seq', 'head'))
- grad_ffn1_norm: float32 [1024], P(('seq', 'head'))
- grad_ffn1_gate: float32 [1024, 4608], P(None, ('seq', 'head'))
- grad_ffn1_up: float32 [1024, 4608], P(None, ('seq', 'head'))
- grad_ffn1_down: float32 [4608, 1024], P(('seq', 'head'))
- grad_attn_norm: float32 [1024], P(('seq', 'head'))
- grad_attn_query: float32 [1024, 1024], P(('seq', 'head'))
- grad_attn_key: float32 [1024, 512], P(('seq', 'head'))
- grad_attn_value: float32 [1024, 512], P(('seq', 'head'))
- grad_qk_gains: float32 [2, 64], replicated
- grad_attn_output: float32 [1024, 1024], P(('seq', 'head'))
- grad_ffn2_norm: float32 [1024], P(('seq', 'head'))
- grad_ffn2_gate: float32 [1024, 4608], P(None, ('seq', 'head'))
- grad_ffn2_up: float32 [1024, 4608], P(None, ('seq', 'head'))
- grad_ffn2_down: float32 [4608, 1024], P(('seq', 'head'))
The draws below stay inside these ranges and needn't reach their ends.
Inputs may be any that keep to these rules, and one draw needn't show every extreme that they name: `doc_starts`: strictly increasing token positions; the first is 0 and the last is 4095.
All inputs are finite; a program needn't handle non-finite values.
Results may differ from the reference program's by a relative error of at most 0.022.
Values may be sent and summed in bfloat16 or wider, within the bound.
No kernel may reach another device: no remote copies, remote signals or barrier semaphores. Data moves between devices by JAX's collectives and lax.ppermute only.
A program may use at most 320 MiB of HBM per device.

```python
import jax
import jax.numpy as jnp
from jax import lax

D = 1024
FF = 4608
HD = 64
TOK_DEV = 128
QDIM = 1024
KVDIM = 512
TOKENS = 4096
N_HEAD = 4


def draw_doc_starts(key, part):
    key = jax.random.fold_in(key, 7)
    edge_rows = TOK_DEV * N_HEAD
    head_key, tail_key = jax.random.split(key)
    head_starts = jnp.sort(jax.random.permutation(head_key, edge_rows - 1)[:3]).astype(jnp.int32) + 1
    tail_starts = jnp.sort(jax.random.permutation(tail_key, edge_rows - 1)[:3]).astype(jnp.int32) + (TOKENS - edge_rows)
    return jnp.concatenate([jnp.zeros((1,), jnp.int32), head_starts, tail_starts, jnp.full((1,), TOKENS - 1, jnp.int32)])


def levels(key, extent, cuts, least, high):
    level = 1.0
    for position, parts in cuts:
        steps = jax.random.uniform(jax.random.fold_in(jax.random.fold_in(key, 6), position), (parts,), jnp.float32, least / len(cuts), high / len(cuts))
        level = level * jnp.repeat(jnp.exp(steps), extent[position] // parts).reshape((-1,) + (1,) * (len(extent) - 1 - position))
    return level


def noise(own_key, shape, deviation, most, shards=(), held_as=jnp.bfloat16):
    values = jax.random.normal(own_key, shape, jnp.float32) * deviation
    if len(shards) > 0:
        values = levels(own_key, shape, shards, -0.22, 0.18) * values
    return jnp.clip(values, min=-most, max=most).astype(held_as)


def setup_inputs(seed: int = 0) -> dict:
    key_of = jax.random.split(jax.random.key(seed), 22)
    return {
        "tokens": noise(key_of[0], (TOKENS, D), 1.0, 6.0, ((0, 32),)),
        "doc_starts": draw_doc_starts(jax.random.fold_in(key_of[21], 71), 0),
        "conv_norm": jnp.clip(1.0 + 0.1 * jax.random.normal(key_of[2], (D,), jnp.float32), 0.5, 1.5).astype(jnp.bfloat16),
        "conv_in": noise(key_of[3], (D, 3 * D), D ** -0.5, 0.1875, ((0, 32),)),
        "conv_kernel": noise(key_of[4], (D, 3), 3 ** -0.5, 3.5, ((0, 32),)),
        "conv_out": noise(key_of[5], (D, D), D ** -0.5, 0.1875, ((0, 32),)),
        "ffn1_norm": jnp.clip(1.0 + 0.1 * jax.random.normal(key_of[6], (D,), jnp.float32), 0.5, 1.5).astype(jnp.bfloat16),
        "ffn1_gate": noise(key_of[7], (D, FF), D ** -0.5, 0.1875, ((1, 32),)),
        "ffn1_up": noise(key_of[8], (D, FF), D ** -0.5, 0.1875, ((1, 32),)),
        "ffn1_down": noise(key_of[9], (FF, D), FF ** -0.5, 0.09375, ((0, 32),)),
        "attn_norm": jnp.clip(1.0 + 0.1 * jax.random.normal(key_of[10], (D,), jnp.float32), 0.5, 1.5).astype(jnp.bfloat16),
        "attn_query": noise(key_of[11], (D, QDIM), D ** -0.5, 0.1875, ((0, 32),)),
        "attn_key": noise(key_of[12], (D, KVDIM), D ** -0.5, 0.1875, ((0, 32),)),
        "attn_value": noise(key_of[13], (D, KVDIM), D ** -0.5, 0.1875, ((0, 32),)),
        "qk_gains": jnp.clip(1.0 + 0.1 * jax.random.normal(key_of[14], (2, HD), jnp.float32), 0.5, 1.5).astype(jnp.bfloat16),
        "attn_output": noise(key_of[15], (QDIM, D), (max(1, QDIM * 16 // TOKENS)) ** -0.5, 3.0, ((0, 32),)),
        "ffn2_norm": jnp.clip(1.0 + 0.1 * jax.random.normal(key_of[16], (D,), jnp.float32), 0.5, 1.5).astype(jnp.bfloat16),
        "ffn2_gate": noise(key_of[17], (D, FF), D ** -0.5, 0.1875, ((1, 32),)),
        "ffn2_up": noise(key_of[18], (D, FF), D ** -0.5, 0.1875, ((1, 32),)),
        "ffn2_down": noise(key_of[19], (FF, D), FF ** -0.5, 0.09375, ((0, 32),)),
        "cotangent": noise(key_of[20], (TOKENS, D), 1.0, 6.0, ((0, 32),)),
    }


EPSILON = 1e-05
ROPE_BASE = 1000000.0

@jax.custom_vjp
def low(v):
    return lax.optimization_barrier(v.astype(jnp.bfloat16)).astype(jnp.float32)

@jax.custom_vjp
def low_back(v):
    return v

def low_keep(v):
    return (low(v), None)

def low_pass(kept, grad):
    return (grad,)

def back_keep(v):
    return (v, None)

def back_low(kept, grad):
    return (low(grad),)
low.defvjp(low_keep, low_pass)
low_back.defvjp(back_keep, back_low)

def rms_norm(values, gain):
    return values * lax.rsqrt(lax.optimization_barrier(jnp.mean(values * values, axis=-1, keepdims=True)) + EPSILON) * gain

def product(left, right):
    return jnp.dot(left, right, precision=lax.Precision.HIGHEST)

def doc_number(positions, starts):
    return lax.optimization_barrier(jnp.sum((starts[None, :] <= positions[:, None]).astype(jnp.int32), axis=1))

def rotate(values, positions):
    half_size = values.shape[-1] // 2
    frequency = jnp.power(jnp.float32(ROPE_BASE), -jnp.arange(half_size, dtype=jnp.float32) * 2.0 / values.shape[-1])
    angles = positions.astype(jnp.float32)[:, None] * frequency[None, :]
    angles = jnp.concatenate([angles, angles], -1)[:, None, :]
    turned = jnp.concatenate([-values[..., half_size:], values[..., :half_size]], -1)
    return values * jnp.cos(angles) + turned * jnp.sin(angles)

def feed_forward(residual, gain, gate_weight, up_weight, down_weight):
    normed = low(rms_norm(residual, gain))
    gate_values = low_back(product(normed, gate_weight))
    up_values = low_back(product(normed, up_weight))
    activation = low(jax.nn.silu(gate_values) * up_values)
    return residual + low_back(product(activation, down_weight))

def conv_block(residual, doc_ids, gain, input_weight, kernel_taps, output_weight):
    model_width = residual.shape[1]
    normed = low(rms_norm(residual, gain))
    projected = low_back(product(normed, input_weight))
    input_gate = projected[:, :model_width]
    output_gate = projected[:, model_width:2 * model_width]
    conv_values = projected[:, 2 * model_width:]
    gated = input_gate * conv_values
    keep_one = (doc_ids[1:] == doc_ids[:-1]).astype(jnp.float32)[:, None]
    keep_two = (doc_ids[2:] == doc_ids[:-2]).astype(jnp.float32)[:, None]
    prev_one = jnp.concatenate([jnp.zeros((1, model_width), jnp.float32), gated[:-1] * keep_one], 0)
    prev_two = jnp.concatenate([jnp.zeros((2, model_width), jnp.float32), gated[:-2] * keep_two], 0)
    conv_sum = kernel_taps[:, 2] * gated + kernel_taps[:, 1] * prev_one + kernel_taps[:, 0] * prev_two
    mixed_rows = low(output_gate * conv_sum)
    return residual + low_back(product(mixed_rows, output_weight))

def attention(queries, keys, values, doc_ids):
    total_rows = queries.shape[0]
    block_rows = 512 if total_rows % 512 == 0 else total_rows
    repeat = queries.shape[1] // keys.shape[1]
    score_scale = queries.shape[2] ** (-0.5)
    key_heads = jnp.repeat(keys, repeat, axis=1).transpose(1, 0, 2)
    value_heads = jnp.repeat(values, repeat, axis=1).transpose(1, 0, 2)
    positions = jnp.arange(total_rows, dtype=jnp.int32)

    def one_block(block_index):
        first_row = block_index * block_rows
        query_block = lax.dynamic_slice_in_dim(queries, first_row, block_rows, 0).transpose(1, 0, 2)
        query_pos = first_row + jnp.arange(block_rows, dtype=jnp.int32)
        query_doc = lax.dynamic_slice_in_dim(doc_ids, first_row, block_rows, 0)
        allowed = ((positions[None, :] <= query_pos[:, None]) & (doc_ids[None, :] == query_doc[:, None]))[None]
        scores = low_back(jnp.einsum('hqd,hkd->hqk', query_block, key_heads, precision=lax.Precision.HIGHEST) * score_scale)
        log_total = jax.nn.logsumexp(scores, axis=-1, where=allowed, keepdims=True)
        weights = jnp.where(allowed, jnp.exp(scores - log_total), 0.0)
        mixed_heads = jnp.einsum('hqk,hkd->qhd', low(weights), value_heads, precision=lax.Precision.HIGHEST)
        return mixed_heads.reshape(block_rows, -1)
    blocks = lax.map(jax.checkpoint(one_block), jnp.arange(total_rows // block_rows, dtype=jnp.int32))
    return blocks.reshape(total_rows, -1)

def forward_pass(residual, doc_starts, conv_norm, conv_in, conv_kernel, conv_out, ffn1_norm, ffn1_gate, ffn1_up, ffn1_down, attn_norm, attn_query, attn_key, attn_value, qk_gains, attn_output, ffn2_norm, ffn2_gate, ffn2_up, ffn2_down):
    total_rows = residual.shape[0]
    head_size = qk_gains.shape[1]
    positions = jnp.arange(total_rows, dtype=jnp.int32)
    doc_ids = doc_number(positions, doc_starts)
    hidden = conv_block(residual, doc_ids, conv_norm, conv_in, conv_kernel, conv_out)
    hidden = feed_forward(hidden, ffn1_norm, ffn1_gate, ffn1_up, ffn1_down)
    normed = low(rms_norm(hidden, attn_norm))
    queries = low_back(product(normed, attn_query)).reshape(total_rows, -1, head_size)
    keys = low_back(product(normed, attn_key)).reshape(total_rows, -1, head_size)
    values = low(low_back(product(normed, attn_value))).reshape(total_rows, -1, head_size)
    queries = low(rotate(rms_norm(queries, qk_gains[0]), positions))
    keys = low(rotate(rms_norm(keys, qk_gains[1]), positions))
    mixed_heads = low(low_back(attention(queries, keys, values, doc_ids)))
    hidden = hidden + low_back(product(mixed_heads, attn_output))
    return feed_forward(hidden, ffn2_norm, ffn2_gate, ffn2_up, ffn2_down)

def reference(tokens, doc_starts, conv_norm, conv_in, conv_kernel, conv_out, ffn1_norm, ffn1_gate, ffn1_up, ffn1_down, attn_norm, attn_query, attn_key, attn_value, qk_gains, attn_output, ffn2_norm, ffn2_gate, ffn2_up, ffn2_down, cotangent):
    weight_list = (conv_norm, conv_in, conv_kernel, conv_out, ffn1_norm, ffn1_gate, ffn1_up, ffn1_down, attn_norm, attn_query, attn_key, attn_value, qk_gains, attn_output, ffn2_norm, ffn2_gate, ffn2_up, ffn2_down)
    floats = tuple((weight.astype(jnp.float32) for weight in weight_list))

    def layer_pair(residual, *params):
        return forward_pass(residual, doc_starts, *params)
    result, pullback = jax.vjp(layer_pair, tokens.astype(jnp.float32), *floats)
    grads = pullback(cotangent.astype(jnp.float32))
    return (result.astype(jnp.bfloat16), grads[0], grads[1], grads[2], grads[3], grads[4], grads[5], grads[6], grads[7], grads[8], grads[9], grads[10], grads[11], grads[12], grads[13], grads[14], grads[15], grads[16], grads[17], grads[18])
```

```python
import functools

import jax
import jax.numpy as jnp
from jax import lax
from jax.experimental import pallas as pl
from jax.experimental.pallas import tpu as pltpu
from jax.sharding import Mesh
from jax.sharding import PartitionSpec as P

EPSILON = 1e-05
ROPE_BASE = 1000000.0
LOG2E = 1.4426950408889634
BF = jnp.bfloat16
F32 = jnp.float32
SWAP = [(0, 1), (1, 0)]
PLANE = ("x", "y", "c")
EVERY = ("z", "x", "y", "c")
TILE = 256


def dot(left, right, left_dim, right_dim):
    return lax.dot_general(
        left, right, (((left_dim,), (right_dim,)), ((), ())), preferred_element_type=F32
    )


def rms_forward(values, gain, axis=-1):
    inverse = lax.rsqrt(jnp.mean(values * values, axis=axis, keepdims=True) + EPSILON)
    return values * inverse * gain, inverse


def rms_backward(values, inverse, gain, gradient, axis=-1):
    unit = values * inverse
    scaled = gradient * gain
    result = inverse * (scaled - unit * jnp.mean(scaled * unit, axis=axis, keepdims=True))
    return result, gradient * unit


def plane_index():
    return lax.axis_index(PLANE)


def reorder(blocks):
    own = plane_index()
    return jnp.stack(
        [lax.dynamic_index_in_dim(blocks, own ^ d, 0, keepdims=False) for d in range(8)]
    )


def gather_plane(piece):
    half = piece.shape[0] // 2
    over_x = lax.ppermute(piece, "x", SWAP)
    over_y = lax.ppermute(piece, "y", SWAP)
    own_c = lax.ppermute(piece, "c", SWAP)
    over_xy0 = lax.ppermute(over_x[:half], "y", SWAP)
    over_xy1 = lax.ppermute(over_y[half:], "x", SWAP)
    over_x_c = lax.ppermute(over_x, "c", SWAP)
    over_y_c = lax.ppermute(over_y, "c", SWAP)
    xy = jnp.concatenate([over_xy0, over_xy1], 0)
    xy_c = lax.ppermute(xy, "c", SWAP)
    return jnp.stack([piece, own_c, over_y, over_y_c, over_x, over_x_c, xy, xy_c])


def scatter_plane(parts):
    rows, width = parts.shape[1:]
    half = width // 2
    parts = parts.reshape(2, 2, 2, rows, width)
    keep = parts[:, :, 0] + lax.ppermute(parts[:, :, 1].astype(BF), "c", SWAP).astype(F32)
    left, right = keep[..., :half], keep[..., half:]
    from_x = lax.ppermute(left[1].astype(BF), "x", SWAP).astype(F32)
    from_y = lax.ppermute(right[:, 1].astype(BF), "y", SWAP).astype(F32)
    left = left[0] + from_x
    right = right[:, 0] + from_y
    left = left[0] + lax.ppermute(left[1].astype(BF), "y", SWAP).astype(F32)
    right = right[0] + lax.ppermute(right[1].astype(BF), "x", SWAP).astype(F32)
    return jnp.concatenate([left, right], -1)


def swap_plane(blocks):
    return lax.all_to_all(blocks, PLANE, split_axis=0, concat_axis=0, tiled=True)


def chain_up(piece, planes):
    arrived = []
    for step in range(1, planes):
        piece = lax.ppermute(piece, "z", [(i, i + 1) for i in range(step - 1, planes - 1)])
        arrived.append(piece)
    return arrived


def chain_down(piece, planes):
    arrived = []
    for step in range(1, planes):
        piece = lax.ppermute(piece, "z", [(i + 1, i) for i in range(planes - step)])
        arrived.append(piece)
    return arrived


def gather_slots(piece, planes):
    z = lax.axis_index("z")
    above, below = chain_down(piece, planes), chain_up(piece, planes)
    slots = [piece]
    for k in range(1, planes):
        slots.append(jnp.where(z >= k, below[k - 1], above[planes - k - 1]))
    return slots


def slots_to_planes(slots):
    planes = len(slots)
    z = lax.axis_index("z")
    stack = jnp.stack(slots)
    return jnp.stack(
        [
            lax.dynamic_index_in_dim(stack, (z - i) % planes, 0, keepdims=False)
            for i in range(planes)
        ]
    )


def planes_to_slots(array):
    planes = array.shape[0]
    z = lax.axis_index("z")
    return [
        lax.dynamic_index_in_dim(array, (z - k) % planes, 0, keepdims=False)
        for k in range(planes)
    ]


def scatter_slots(slots):
    planes = len(slots)
    low = [s.astype(BF) for s in slots]
    total = slots[0].astype(F32)
    carried = None
    for r in range(planes - 1, 0, -1):
        value = low[planes - r]
        if carried is not None:
            value = (slots[planes - r].astype(F32) + carried.astype(F32)).astype(BF)
        carried = lax.ppermute(value, "z", [(i, i + 1) for i in range(planes - r)])
    if carried is not None:
        total = total + carried.astype(F32)
    carried = None
    for r in range(planes - 1, 0, -1):
        value = low[r]
        if carried is not None:
            value = (slots[r].astype(F32) + carried.astype(F32)).astype(BF)
        carried = lax.ppermute(value, "z", [(i, i - 1) for i in range(r, planes)])
    if carried is not None:
        total = total + carried.astype(F32)
    return total


def gather_rows(weight, planes):
    rows, width = weight.shape
    by_plane = slots_to_planes(gather_slots(weight, planes))
    blocks = reorder(gather_plane(by_plane.reshape(planes * rows, width)))
    return (
        blocks.reshape(8, planes, rows, width).transpose(1, 0, 2, 3).reshape(-1, width)
    )


def scatter_rows(grad, planes):
    width = grad.shape[1]
    rows = grad.shape[0] // (8 * planes)
    blocks = grad.reshape(planes, 8, rows, width).transpose(1, 0, 2, 3)
    blocks = reorder(blocks.reshape(8, planes * rows, width))
    mine = scatter_plane(blocks).reshape(planes, rows, width)
    return scatter_slots(planes_to_slots(mine))


META = 18


def tile_masks(meta, key_tile, query_tile):
    key_first = meta[2 + key_tile]
    key_last = key_first + (TILE - 1)
    query_first = meta[6 + query_tile]
    query_last = query_first + (TILE - 1)
    start_first = meta[10 + query_tile]
    start_last = meta[14 + query_tile]
    some = (key_last >= start_first) & (key_first <= query_last) & (meta[0] > 0)
    whole = (key_first >= start_last) & (key_last <= query_first)
    return some, whole


def allowed_mask(meta, key_tile, query_rows, start_rows, shape):
    row = lax.broadcasted_iota(jnp.int32, shape, 0)
    key_pos = meta[2 + key_tile] + (row ^ meta[1])
    return (key_pos <= query_rows) & (key_pos >= start_rows)


def forward_kernel(meta, pair, query, rows, acc_in, total_in, acc, total, keys):
    head = pair.shape[0] // 2
    tiles = pair.shape[1] // TILE
    wide = query.shape[1] // tiles
    acc[...] = acc_in[...]
    total[...] = total_in[...]

    @pl.when(meta[0] > 0)
    def _():
        keys[...] = pair[:head, :].astype(F32).T.astype(BF)
        for q in range(tiles):
            columns = slice(q * wide, (q + 1) * wide)
            for k in range(tiles):
                some, whole = tile_masks(meta, k, q)

                def work(masked, q=q, k=k, columns=columns):
                    scores = dot(keys[k * TILE : (k + 1) * TILE, :], query[:, columns], 1, 0)
                    terms = jnp.exp2(scores * LOG2E)
                    if masked:
                        mask = allowed_mask(
                            meta, k, rows[0:1, columns], rows[1:2, columns], terms.shape
                        )
                        terms = jnp.where(mask, terms, 0.0)
                    total[0:1, columns] += jnp.sum(terms, 0, keepdims=True)
                    acc[:, columns] += dot(
                        pair[head:, k * TILE : (k + 1) * TILE], terms.astype(BF), 1, 0
                    )

                pl.when(some & whole)(functools.partial(work, False))
                pl.when(some & jnp.logical_not(whole))(functools.partial(work, True))


def attend(meta, pair, query, rows, acc, total):
    head = query.shape[0]
    count = pair.shape[1]
    vmem = pl.BlockSpec(memory_space=pltpu.VMEM)
    return pl.pallas_call(
        forward_kernel,
        out_shape=(
            jax.ShapeDtypeStruct(acc.shape, F32),
            jax.ShapeDtypeStruct(total.shape, F32),
        ),
        in_specs=[pl.BlockSpec(memory_space=pltpu.SMEM)] + [vmem] * 5,
        out_specs=(vmem, vmem),
        scratch_shapes=[pltpu.VMEM((count, head), BF)],
        compiler_params=pltpu.CompilerParams(vmem_limit_bytes=32 * 1024 * 1024),
        cost_estimate=pl.CostEstimate(
            flops=4 * count * query.shape[1] * head,
            bytes_accessed=2 * (pair.size + query.size) + 8 * acc.size,
            transcendentals=count * query.shape[1],
        ),
    )(meta, pair, query, rows, acc, total)


def backward_kernel(
    meta, pair, query, out_grad, rows, log_total, delta, query_in, query_grad, pair_grad, keys, values
):
    head = pair.shape[0] // 2
    tiles = pair.shape[1] // TILE
    wide = query.shape[1] // tiles
    query_grad[...] = query_in[...]
    pair_grad[...] = jnp.zeros(pair_grad.shape, F32)

    @pl.when(meta[0] > 0)
    def _():
        keys[...] = pair[:head, :].astype(F32).T.astype(BF)
        values[...] = pair[head:, :].astype(F32).T.astype(BF)
        for k in range(tiles):
            span = slice(k * TILE, (k + 1) * TILE)
            for q in range(tiles):
                columns = slice(q * wide, (q + 1) * wide)
                some, whole = tile_masks(meta, k, q)

                def work(masked, k=k, columns=columns, span=span):
                    scores = dot(keys[span, :], query[:, columns], 1, 0)
                    weights = jnp.exp2(scores * LOG2E - log_total[0:1, columns])
                    if masked:
                        mask = allowed_mask(
                            meta, k, rows[0:1, columns], rows[1:2, columns], weights.shape
                        )
                        weights = jnp.where(mask, weights, 0.0)
                    weight_grad = dot(values[span, :], out_grad[:, columns], 1, 0)
                    score_grad = (weights * (weight_grad - delta[0:1, columns])).astype(BF)
                    pair_grad[span, :head] += dot(score_grad, query[:, columns], 1, 1)
                    pair_grad[span, head:] += dot(weights.astype(BF), out_grad[:, columns], 1, 1)
                    query_grad[:, columns] += dot(pair[:head, span], score_grad, 1, 0)

                pl.when(some & whole)(functools.partial(work, False))
                pl.when(some & jnp.logical_not(whole))(functools.partial(work, True))


def attend_back(meta, pair, query, out_grad, rows, log_total, delta, query_grad):
    head = query.shape[0]
    count = pair.shape[1]
    vmem = pl.BlockSpec(memory_space=pltpu.VMEM)
    return pl.pallas_call(
        backward_kernel,
        out_shape=(
            jax.ShapeDtypeStruct(query_grad.shape, F32),
            jax.ShapeDtypeStruct((count, 2 * head), F32),
        ),
        in_specs=[pl.BlockSpec(memory_space=pltpu.SMEM)] + [vmem] * 7,
        out_specs=(vmem, vmem),
        scratch_shapes=[pltpu.VMEM((count, head), BF), pltpu.VMEM((count, head), BF)],
        compiler_params=pltpu.CompilerParams(vmem_limit_bytes=32 * 1024 * 1024),
        cost_estimate=pl.CostEstimate(
            flops=10 * count * query.shape[1] * head,
            bytes_accessed=2 * (pair.size + 2 * query.size) + 8 * query.size,
            transcendentals=count * query.shape[1],
        ),
    )(meta, pair, query, out_grad, rows, log_total, delta, query_grad)


def ffn_weights(gate, up, down, planes):
    pack = jnp.concatenate([gate.T, up.T, down], 0)
    slots = gather_slots(pack, planes)
    unit = down.shape[0]
    both = jnp.stack([s[: 2 * unit] for s in slots])
    low = jnp.stack([s[2 * unit :] for s in slots])
    return both.reshape(-1, both.shape[-1]), low.reshape(-1, low.shape[-1])


def ffn_up(normed, both, planes):
    hidden = dot(both, normed, 1, 1)
    hidden = hidden.reshape(planes, 2, -1, hidden.shape[-1])
    gate, up = hidden[:, 0], hidden[:, 1]
    act = (jax.nn.silu(gate) * up).astype(BF)
    return gate, up, act.reshape(-1, act.shape[-1])


def ffn_back(act_grad, gate, up, normed, both):
    act_grad = act_grad.reshape(gate.shape)
    sig = jax.nn.sigmoid(gate)
    gate_grad = (act_grad * up * sig * (1.0 + gate * (1.0 - sig))).astype(BF)
    up_grad = (act_grad * gate * sig).astype(BF)
    hidden_grad = jnp.stack([gate_grad, up_grad], 1).reshape(-1, gate.shape[-1])
    return hidden_grad, dot(hidden_grad, both, 0, 0)


def ffn_shards(both_grad, down_grad, planes):
    width = down_grad.shape[-1]
    both_grad = both_grad.reshape(planes, -1, width)
    down_grad = down_grad.reshape(planes, -1, width)
    slots = [jnp.concatenate([both_grad[k], down_grad[k]], 0) for k in range(planes)]
    mine = scatter_slots(slots)
    unit = down_grad.shape[1]
    return mine[:unit].T, mine[unit : 2 * unit].T, mine[2 * unit :]


def body(
    tokens,
    doc_starts,
    conv_norm,
    conv_in,
    conv_kernel,
    conv_out,
    ffn1_norm,
    ffn1_gate,
    ffn1_up_weight,
    ffn1_down,
    attn_norm,
    attn_query,
    attn_key,
    attn_value,
    qk_gains,
    attn_output,
    ffn2_norm,
    ffn2_gate,
    ffn2_up_weight,
    ffn2_down,
    cotangent,
):
    planes = lax.axis_size("z")
    z = lax.axis_index("z")
    own = plane_index()
    rows, width = tokens.shape
    count = 8 * rows
    owned = conv_norm.shape[0]
    head = qk_gains.shape[1]
    heads = attn_query.shape[1] // (8 * head)
    part = width // 8
    devices = 8 * planes

    block_pos = (own ^ jnp.arange(8, dtype=jnp.int32)) * rows + z * count
    positions = (block_pos[:, None] + jnp.arange(rows, dtype=jnp.int32)[None, :]).reshape(-1)
    starts = jnp.max(
        jnp.where(doc_starts[None, :] <= positions[:, None], doc_starts[None, :], 0), 1
    )
    keep_one = (positions - 1 >= starts).astype(F32).reshape(8, rows, 1)
    keep_two = (positions - 2 >= starts).astype(F32).reshape(8, rows, 1)

    small = jnp.concatenate(
        [
            jnp.stack([conv_norm, ffn1_norm, attn_norm, ffn2_norm], 0),
            conv_kernel.T,
            jnp.zeros((1, owned), BF),
        ],
        0,
    )
    small = lax.all_to_all(
        jnp.broadcast_to(small[None], (devices, 8, owned)),
        EVERY,
        split_axis=0,
        concat_axis=0,
        tiled=True,
    )
    small = small.transpose(1, 0, 2).reshape(8, width).astype(F32)
    conv_gain, ffn1_gain, attn_gain, ffn2_gain = (small[i : i + 1] for i in range(4))
    taps = lax.dynamic_slice(small[4:7], (0, own * part), (3, part))[:, None, None, :]

    in_columns = jnp.concatenate(
        [
            conv_in.reshape(owned, 3, 8, part).transpose(2, 0, 1, 3).reshape(8, owned, 3 * part),
            attn_query.reshape(owned, 8, -1).transpose(1, 0, 2),
            attn_key.reshape(owned, 8, -1).transpose(1, 0, 2),
            attn_value.reshape(owned, 8, -1).transpose(1, 0, 2),
        ],
        2,
    )
    in_columns = swap_plane(in_columns).reshape(8 * owned, -1)
    in_columns = slots_to_planes(gather_slots(in_columns, planes)).reshape(width, -1)
    conv_weight = in_columns[:, : 3 * part]
    qkv_weight = in_columns[:, 3 * part :]

    raw = gather_plane(tokens).reshape(count, width).astype(F32)
    conv_out_all = gather_rows(conv_out, planes)
    both_one, down_one = ffn_weights(ffn1_gate, ffn1_up_weight, ffn1_down, planes)
    attn_output_all = gather_rows(attn_output, planes)
    both_two, down_two = ffn_weights(ffn2_gate, ffn2_up_weight, ffn2_down, planes)
    cotangent_all = gather_plane(cotangent).reshape(count, width)

    residual = tokens.astype(F32)
    normed_conv, raw_inverse = rms_forward(raw, conv_gain)
    normed_conv = normed_conv.astype(BF)
    projected = dot(normed_conv, conv_weight, 1, 0).reshape(8, rows, 3 * part)
    in_gate = projected[..., :part]
    out_gate = projected[..., part : 2 * part]
    conv_values = projected[..., 2 * part :]
    gated = in_gate * conv_values
    tails = reorder(gated[:, rows - 2 :])
    rim = lax.ppermute(tails[7], "z", [(i, i + 1) for i in range(planes - 1)])
    before = reorder(jnp.concatenate([rim[None], tails[:7]], 0))
    prev_one = jnp.concatenate([before[:, 1:], gated[:, :-1]], 1) * keep_one
    prev_two = jnp.concatenate([before, gated[:, :-2]], 1) * keep_two
    conv_sum = taps[2] * gated + taps[1] * prev_one + taps[0] * prev_two
    mixed = (out_gate * conv_sum).astype(BF)
    mixed_rows = swap_plane(reorder(mixed)).transpose(1, 0, 2).reshape(rows, width)
    hidden_one = residual + dot(mixed_rows, conv_out_all, 1, 0)

    normed, inverse_one = rms_forward(hidden_one, ffn1_gain)
    normed_one = gather_plane(normed.astype(BF)).reshape(count, width)
    gate_one, up_one, act_one = ffn_up(normed_one, both_one, planes)
    hidden_two = hidden_one + scatter_plane(
        dot(act_one, down_one, 0, 0).reshape(8, rows, width)
    )

    normed, inverse_attn = rms_forward(hidden_two, attn_gain)
    normed_attn = gather_plane(normed.astype(BF)).reshape(count, width)
    raw_qkv = dot(qkv_weight, normed_attn, 0, 1)
    query_raw = raw_qkv[: heads * head].reshape(heads, head, count)
    key_raw = raw_qkv[heads * head : (heads + 1) * head][None]
    value_low = raw_qkv[(heads + 1) * head :].astype(BF)
    gains = qk_gains.astype(F32)
    query_gain, key_gain = gains[0][None, :, None], gains[1][None, :, None]
    half = head // 2
    frequency = jnp.power(
        jnp.float32(ROPE_BASE), -jnp.arange(half, dtype=F32) * 2.0 / head
    )
    angles = frequency[:, None] * positions.astype(F32)[None, :]
    cosine, sine = jnp.cos(angles)[None], jnp.sin(angles)[None]

    def rope(v):
        first, second = v[:, :half], v[:, half:]
        return jnp.concatenate(
            [first * cosine - second * sine, second * cosine + first * sine], 1
        )

    def rope_back(g):
        first, second = g[:, :half], g[:, half:]
        return jnp.concatenate(
            [first * cosine + second * sine, second * cosine - first * sine], 1
        )

    query_unit, query_inverse = rms_forward(query_raw, query_gain, 1)
    key_unit, key_inverse = rms_forward(key_raw, key_gain, 1)
    query_low = rope(query_unit).astype(BF)
    key_low = rope(key_unit).astype(BF)[0]

    tiles = count // TILE

    def lay(v):
        features = v.shape[1]
        v = v.reshape(heads, features, tiles, TILE).transpose(1, 2, 0, 3)
        return v.reshape(features, heads * count)

    def unlay(v):
        features = v.shape[0]
        v = v.reshape(features, tiles, heads, TILE).transpose(2, 0, 1, 3)
        return v.reshape(heads, features, count)

    query_cols = lay((query_low.astype(F32) * (head**-0.5)).astype(BF))
    row_info = lay(jnp.broadcast_to(jnp.stack([positions, starts])[None], (heads, 2, count)))
    tile_first = (own // 2 ^ jnp.arange(tiles, dtype=jnp.int32)) * TILE
    tile_starts = jnp.max(
        jnp.where(
            doc_starts[None, :]
            <= (z * count + tile_first[:, None, None] + jnp.array([[0], [TILE - 1]])),
            doc_starts[None, None, :],
            0,
        ),
        2,
    )
    core = (own % 2) * rows

    def meta_of(step):
        return jnp.concatenate(
            [
                jnp.stack([(z >= step).astype(jnp.int32), core]),
                (z - step) * count + tile_first,
                z * count + tile_first,
                tile_starts[:, 0],
                tile_starts[:, 1],
            ]
        ).astype(jnp.int32)

    metas = [meta_of(step) for step in range(planes)]
    pair = jnp.concatenate([key_low, value_low], 0)
    pairs = [pair] + chain_up(pair, planes)
    acc = jnp.zeros((head, heads * count), F32)
    total = jnp.zeros((1, heads * count), F32)
    for step in range(planes):
        acc, total = attend(metas[step], pairs[step], query_cols, row_info, acc, total)
    log_total = jnp.log2(total)
    mixed_heads = acc / total
    head_low = unlay(mixed_heads).astype(BF)
    sent = head_low.reshape(heads * head, 8, rows).transpose(1, 2, 0)
    attended = swap_plane(reorder(sent)).transpose(1, 0, 2).reshape(rows, -1)
    hidden_three = hidden_two + dot(attended, attn_output_all, 1, 0)

    normed, inverse_two = rms_forward(hidden_three, ffn2_gain)
    normed_two = gather_plane(normed.astype(BF)).reshape(count, width)
    act_grad_two = dot(down_two, cotangent_all, 1, 1)
    gate_two, up_two, act_two = ffn_up(normed_two, both_two, planes)
    hidden_grad, partial = ffn_back(act_grad_two, gate_two, up_two, normed_two, both_two)
    normed_grad = scatter_plane(partial.reshape(8, rows, width))
    residual_grad, gain_rows_two = rms_backward(hidden_three, inverse_two, ffn2_gain, normed_grad)
    gradient = cotangent.astype(F32) + residual_grad
    hidden_four = hidden_three + scatter_plane(
        dot(act_two, down_two, 0, 0).reshape(8, rows, width)
    )
    output = hidden_four.astype(BF)
    grad_ffn2 = ffn_shards(
        dot(hidden_grad, normed_two, 1, 0), dot(act_two, cotangent_all, 1, 0), planes
    )

    gradient_low = gradient.astype(BF)
    attended_grad = dot(gradient_low, attn_output_all, 1, 1).astype(BF)
    sent = attended_grad.reshape(rows, 8, -1).transpose(1, 0, 2)
    head_grad = reorder(swap_plane(sent)).reshape(count, -1).T
    head_grad = head_grad.reshape(heads, head, count)
    out_grad = lay(head_grad)
    delta = jnp.sum(out_grad.astype(F32) * mixed_heads, 0, keepdims=True)
    grad_attn_output = scatter_rows(dot(attended, gradient_low, 0, 0), planes)

    query_grad = jnp.zeros((head, heads * count), F32)
    carried = None
    for step in range(planes - 1, -1, -1):
        query_grad, pair_grad = attend_back(
            metas[step],
            pairs[step],
            query_cols,
            out_grad,
            row_info,
            log_total,
            delta,
            query_grad,
        )
        if carried is not None:
            pair_grad = pair_grad + carried.astype(F32)
        if step > 0:
            carried = lax.ppermute(
                pair_grad.astype(BF), "z", [(i, i - 1) for i in range(step, planes)]
            )
    pair_grad = pair_grad.T
    query_tok = unlay(query_grad) * (head**-0.5)
    query_raw_grad, query_gain_rows = rms_backward(
        query_raw, query_inverse, query_gain, rope_back(query_tok), 1
    )
    key_raw_grad, key_gain_rows = rms_backward(
        key_raw, key_inverse, key_gain, rope_back(pair_grad[None, :head]), 1
    )
    qk_rows = jnp.stack(
        [jnp.sum(query_gain_rows, (0, 2)), jnp.sum(key_gain_rows, (0, 2))]
    ).reshape(-1)
    qkv_grad = jnp.concatenate(
        [
            query_raw_grad.reshape(heads * head, count).astype(BF),
            key_raw_grad[0].astype(BF),
            pair_grad[head:].astype(BF),
        ],
        0,
    )
    normed_grad = scatter_plane(dot(qkv_grad, qkv_weight, 0, 1).reshape(8, rows, width))
    residual_grad, gain_rows_attn = rms_backward(hidden_two, inverse_attn, attn_gain, normed_grad)
    gradient = gradient + residual_grad
    qkv_weight_grad = dot(normed_attn, qkv_grad, 0, 1)

    def in_shards(grad):
        mine = scatter_slots(planes_to_slots(grad.reshape(planes, 8 * owned, -1)))
        mine = swap_plane(mine.astype(BF).reshape(8, owned, -1)).astype(F32)
        return mine.transpose(1, 0, 2)

    grad_qkv = in_shards(qkv_weight_grad)

    gradient_low = gather_plane(gradient.astype(BF)).reshape(count, width)
    act_grad_one = dot(down_one, gradient_low, 1, 1)
    hidden_grad, partial = ffn_back(act_grad_one, gate_one, up_one, normed_one, both_one)
    normed_grad = scatter_plane(partial.reshape(8, rows, width))
    residual_grad, gain_rows_one = rms_backward(hidden_one, inverse_one, ffn1_gain, normed_grad)
    gradient = gradient + residual_grad
    grad_ffn1 = ffn_shards(
        dot(hidden_grad, normed_one, 1, 0), dot(act_one, gradient_low, 1, 0), planes
    )

    gradient_low = gradient.astype(BF)
    mixed_grad = dot(gradient_low, conv_out_all, 1, 1).astype(BF)
    mixed_grad = swap_plane(mixed_grad.reshape(rows, 8, part).transpose(1, 0, 2))
    mixed_grad = reorder(mixed_grad).astype(F32)
    grad_conv_out = scatter_rows(dot(mixed_rows, gradient_low, 0, 0), planes)
    out_gate_grad = mixed_grad * conv_sum
    conv_grad = mixed_grad * out_gate
    kernel_grad = jnp.stack(
        [
            jnp.sum(conv_grad * prev_two, (0, 1)),
            jnp.sum(conv_grad * prev_one, (0, 1)),
            jnp.sum(conv_grad * gated, (0, 1)),
        ],
        1,
    )
    back_one = taps[1] * conv_grad * keep_one
    back_two = taps[0] * conv_grad * keep_two
    fronts = reorder(jnp.concatenate([back_one[:, :1], back_two[:, :2]], 1))
    rim = lax.ppermute(fronts[0], "z", [(i + 1, i) for i in range(planes - 1)])
    after = reorder(jnp.concatenate([fronts[1:], rim[None]], 0))
    gated_grad = (
        taps[2] * conv_grad
        + jnp.concatenate([back_one[:, 1:], after[:, :1]], 1)
        + jnp.concatenate([back_two[:, 2:], after[:, 1:]], 1)
    )
    projected_grad = (
        jnp.concatenate([gated_grad * conv_values, out_gate_grad, gated_grad * in_gate], 2)
        .astype(BF)
        .reshape(count, 3 * part)
    )
    partial = dot(projected_grad, conv_weight, 1, 1)
    gain_conv = jnp.sum(partial * (raw * raw_inverse), 0)
    normed_grad = scatter_plane(partial.reshape(8, rows, width))
    inverse = lax.rsqrt(jnp.mean(residual * residual, axis=-1, keepdims=True) + EPSILON)
    residual_grad, _ = rms_backward(residual, inverse, conv_gain, normed_grad)
    grad_tokens = gradient + residual_grad
    grad_conv_in = in_shards(dot(normed_conv, projected_grad, 0, 0))

    kernel_all = lax.dynamic_update_slice(jnp.zeros((width, 3), F32), kernel_grad, (own * part, 0))
    small_grads = jnp.concatenate(
        [
            gain_conv.reshape(devices, owned),
            jnp.sum(gain_rows_one, 0).reshape(devices, owned),
            jnp.sum(gain_rows_attn, 0).reshape(devices, owned),
            jnp.sum(gain_rows_two, 0).reshape(devices, owned),
            kernel_all.reshape(devices, 3 * owned),
            jnp.broadcast_to(qk_rows[None], (devices, qk_rows.shape[0])),
        ],
        1,
    )
    small_grads = lax.all_to_all(
        small_grads[:, None, :], EVERY, split_axis=0, concat_axis=0, tiled=True
    )
    small_grads = jnp.sum(small_grads, (0, 1))
    grad_norms = [small_grads[i * owned : (i + 1) * owned] for i in range(4)]
    grad_kernel = small_grads[4 * owned : 7 * owned].reshape(owned, 3)
    grad_gains = small_grads[7 * owned :].reshape(2, head)

    query_part = heads * head
    return (
        output,
        grad_tokens,
        grad_norms[0],
        grad_conv_in.reshape(owned, 8, 3, part).transpose(0, 2, 1, 3).reshape(owned, 3 * width),
        grad_kernel,
        grad_conv_out,
        grad_norms[1],
        grad_ffn1[0],
        grad_ffn1[1],
        grad_ffn1[2],
        grad_norms[2],
        grad_qkv[:, :, :query_part].reshape(owned, -1),
        grad_qkv[:, :, query_part : query_part + head].reshape(owned, -1),
        grad_qkv[:, :, query_part + head :].reshape(owned, -1),
        grad_gains,
        grad_attn_output,
        grad_norms[3],
        grad_ffn2[0],
        grad_ffn2[1],
        grad_ffn2[2],
    )


def solution(mesh):
    seq, heads = mesh.shape["seq"], mesh.shape["head"]
    grid = Mesh(mesh.devices.reshape(seq // 2, 2, heads // 2, 2), EVERY)
    lead, both, last = P(EVERY), P(EVERY, None), P(None, EVERY)
    return jax.shard_map(
        body,
        mesh=grid,
        in_specs=(
            both,
            P(),
            lead,
            both,
            both,
            both,
            lead,
            last,
            last,
            both,
            lead,
            both,
            both,
            both,
            P(),
            both,
            lead,
            last,
            last,
            both,
            both,
        ),
        out_specs=(
            both,
            both,
            lead,
            both,
            both,
            both,
            lead,
            last,
            last,
            both,
            lead,
            both,
            both,
            both,
            P(),
            both,
            lead,
            last,
            last,
            both,
        ),
        check_vma=False,
    )
```

```python
import functools

import jax
import jax.numpy as jnp
from jax import lax
from jax.experimental import pallas as pl
from jax.experimental.pallas import tpu as pltpu
from jax.sharding import Mesh
from jax.sharding import PartitionSpec as P

EPSILON = 1e-05
ROPE_BASE = 1000000.0
LOG2E = 1.4426950408889634
BF = jnp.bfloat16
F32 = jnp.float32
PLANE = ("x", "y", "c")
EVERY = ("z", "x", "y", "c")
TILE = 256


def dot(left, right, left_dim, right_dim):
    return lax.dot_general(
        left, right, (((left_dim,), (right_dim,)), ((), ())), preferred_element_type=F32
    )


def rms_forward(values, gain, axis=-1):
    inverse = lax.rsqrt(jnp.mean(values * values, axis=axis, keepdims=True) + EPSILON)
    return values * inverse * gain, inverse


def rms_backward(values, inverse, gain, gradient, axis=-1):
    unit = values * inverse
    scaled = gradient * gain
    result = inverse * (scaled - unit * jnp.mean(scaled * unit, axis=axis, keepdims=True))
    return result, gradient * unit


def plane_index():
    return lax.axis_index(PLANE)


def swap_all(blocks):
    return lax.all_to_all(blocks, EVERY, split_axis=0, concat_axis=0, tiled=True)


SWAP = [(0, 1), (1, 0)]


def core_swap(block):
    return lax.ppermute(block, "c", SWAP)


def chip_swap(block, distance):
    return lax.ppermute(block, ("x", "y"), [(i, i ^ distance) for i in range(4)])


def join_kernel(take, *refs):
    pieces, outs = refs[: -len(take)], refs[-len(take) :]
    first = 0
    for rows, out in zip(take, outs):
        for i, piece in enumerate(pieces):
            out[i * rows : (i + 1) * rows, :] = piece[first : first + rows, :]
        first += rows


def join(pieces, take=None):
    rows, width = pieces[0].shape
    take = take or (rows,)
    vmem = pl.BlockSpec(memory_space=pltpu.VMEM)
    out = pl.pallas_call(
        functools.partial(join_kernel, take),
        out_shape=tuple(
            jax.ShapeDtypeStruct((len(pieces) * t, width), pieces[0].dtype) for t in take
        ),
        in_specs=[vmem] * len(pieces),
        out_specs=(vmem,) * len(take),
        compiler_params=pltpu.CompilerParams(vmem_limit_bytes=16 * 1024 * 1024),
        cost_estimate=pl.CostEstimate(
            flops=0, bytes_accessed=4 * len(pieces) * rows * width, transcendentals=0
        ),
    )(*pieces)
    return out if len(take) > 1 else out[0]


def pack_kernel(gate, up, down, *rest):
    unit = down.shape[0]
    out = rest[-1]
    out[:unit, :] = gate[...].astype(F32).T.astype(BF)
    out[unit : 2 * unit, :] = up[...].astype(F32).T.astype(BF)
    out[2 * unit : 3 * unit, :] = down[...]
    if len(rest) > 1:
        out[3 * unit :, :] = rest[0][...]


def pack(gate, up, down, *extra):
    unit, width = down.shape
    rows = 3 * unit + sum(e.shape[0] for e in extra)
    if unit % 16 or rows % 16:
        return jnp.concatenate([gate.T, up.T, down, *extra], 0)
    vmem = pl.BlockSpec(memory_space=pltpu.VMEM)
    return pl.pallas_call(
        pack_kernel,
        out_shape=jax.ShapeDtypeStruct((rows, width), BF),
        in_specs=[vmem] * (3 + len(extra)),
        out_specs=vmem,
        compiler_params=pltpu.CompilerParams(vmem_limit_bytes=16 * 1024 * 1024),
        cost_estimate=pl.CostEstimate(
            flops=0, bytes_accessed=12 * unit * width, transcendentals=0
        ),
    )(gate, up, down, *extra)


def unpack_kernel(both, gate, up):
    unit = both.shape[0] // 2
    gate[...] = both[:unit, :].astype(F32).T
    up[...] = both[unit:, :].astype(F32).T


def unpack(both):
    unit, width = both.shape[0] // 2, both.shape[1]
    if unit % 16:
        both = both.astype(F32)
        return both[:unit].T, both[unit:].T
    vmem = pl.BlockSpec(memory_space=pltpu.VMEM)
    out = jax.ShapeDtypeStruct((width, unit), F32)
    return pl.pallas_call(
        unpack_kernel,
        out_shape=(out, out),
        in_specs=[vmem],
        out_specs=(vmem, vmem),
        compiler_params=pltpu.CompilerParams(vmem_limit_bytes=16 * 1024 * 1024),
        cost_estimate=pl.CostEstimate(
            flops=0, bytes_accessed=12 * unit * width, transcendentals=0
        ),
    )(both)


def lanes_kernel(splits, blocks, *outs):
    planes = blocks.shape[0] // 8
    for j in range(8):
        block = blocks[j].astype(F32)
        for k in range(1, planes):
            block = block + blocks[8 * k + j].astype(F32)
        for first, size, out, place in splits(j, outs):
            out[:, place : place + size] = block[:, first : first + size]


def lanes_back(blocks, widths, splits):
    vmem = pl.BlockSpec(memory_space=pltpu.VMEM)
    rows = blocks.shape[1]
    return pl.pallas_call(
        functools.partial(lanes_kernel, splits),
        out_shape=tuple(jax.ShapeDtypeStruct((rows, w), F32) for w in widths),
        in_specs=[vmem],
        out_specs=(vmem,) * len(widths),
        compiler_params=pltpu.CompilerParams(vmem_limit_bytes=16 * 1024 * 1024),
        cost_estimate=pl.CostEstimate(
            flops=0, bytes_accessed=4 * blocks.size, transcendentals=0
        ),
    )(blocks)


def spread_kernel(weight, small, out):
    part = weight.shape[1] // 24
    for j in range(8):
        for i in range(3):
            first = (i * 8 + j) * part
            out[j, :, i * part : (i + 1) * part] = weight[:, first : first + part]
        out[j, :, 3 * part :] = small[...]
    for k in range(8, out.shape[0]):
        out[k] = out[k % 8]


def spread(weight, small, devices):
    rows = weight.shape[0]
    width = weight.shape[1] // 8 + small.shape[1]
    if rows % 16:
        columns = jnp.concatenate(
            [
                weight.reshape(rows, 3, 8, -1).transpose(2, 0, 1, 3).reshape(8, rows, -1),
                jnp.broadcast_to(small[None], (8,) + small.shape),
            ],
            2,
        )
        return jnp.tile(columns, (devices // 8, 1, 1))
    vmem = pl.BlockSpec(memory_space=pltpu.VMEM)
    return pl.pallas_call(
        spread_kernel,
        out_shape=jax.ShapeDtypeStruct((devices, rows, width), BF),
        in_specs=[vmem] * 2,
        out_specs=vmem,
        compiler_params=pltpu.CompilerParams(vmem_limit_bytes=16 * 1024 * 1024),
        cost_estimate=pl.CostEstimate(
            flops=0, bytes_accessed=4 * devices * rows * width, transcendentals=0
        ),
    )(weight, small)


def gather_plane(piece):
    return gather_cores([piece] + [chip_swap(piece, d) for d in (1, 2, 3)])


def gather_cores(chips, take=None):
    return join([v for chip in chips for v in (chip, core_swap(chip))], take)


def place_kernel(cut, z, *refs):
    planes = len(refs) - 2
    pieces, first, second = refs[:planes], refs[-2], refs[-1]
    rest = pieces[0].shape[0] - cut
    for t, piece in enumerate(pieces):
        k = (z[0] - t + planes) % planes
        first[pl.ds(pl.multiple_of(k * cut, cut), cut), :] = piece[:cut, :]
        second[pl.ds(pl.multiple_of(k * rest, rest), rest), :] = piece[cut:, :]


def place(pieces, cut):
    planes = len(pieces)
    rows, width = pieces[0].shape
    z = lax.axis_index("z")
    if cut % 16 or rows % 16:
        stack = jnp.stack(pieces)
        order = [
            lax.dynamic_index_in_dim(stack, (z - k) % planes, 0, keepdims=False)
            for k in range(planes)
        ]
        return (
            jnp.concatenate([v[:cut] for v in order], 0),
            jnp.concatenate([v[cut:] for v in order], 0),
        )
    vmem = pl.BlockSpec(memory_space=pltpu.VMEM)
    return pl.pallas_call(
        functools.partial(place_kernel, cut),
        out_shape=(
            jax.ShapeDtypeStruct((planes * cut, width), BF),
            jax.ShapeDtypeStruct((planes * (rows - cut), width), BF),
        ),
        in_specs=[pl.BlockSpec(memory_space=pltpu.SMEM)] + [vmem] * planes,
        out_specs=(vmem, vmem),
        compiler_params=pltpu.CompilerParams(vmem_limit_bytes=16 * 1024 * 1024),
        cost_estimate=pl.CostEstimate(
            flops=0, bytes_accessed=4 * planes * rows * width, transcendentals=0
        ),
    )(z.reshape(1).astype(jnp.int32), *pieces)


def scatter_plane(parts):
    low = parts.astype(BF).reshape(4, 2, parts.shape[0] // 8, parts.shape[1])
    mine = low[:, 0].astype(F32) + core_swap(low[:, 1]).astype(F32)
    sent = mine.astype(BF)
    total = mine[0]
    for d in (1, 2, 3):
        total = total + chip_swap(sent[d], d).astype(F32)
    return total


def rows_of_plane_index(first, second):
    planes = lax.axis_size("z")
    piece = jnp.concatenate([first, second], 0)
    got = []
    for t in range(planes):
        pairs = [
            (j * planes + k, (k + t) % planes * 8 + j) for j in range(8) for k in range(planes)
        ]
        got.append(lax.ppermute(piece, EVERY, pairs))
    return got


def rows_to_planes(terms):
    planes, rows, width = terms.shape
    if planes >= 8:
        sent = terms.reshape(planes // 8, 8, rows, width).transpose(1, 0, 2, 3)
        got = lax.all_to_all(sent, PLANE, split_axis=0, concat_axis=0, tiled=True)
        return got.reshape(planes, rows, width)
    share = 8 // planes
    sent = jnp.concatenate([terms] * share, 0)
    got = lax.all_to_all(sent, PLANE, split_axis=0, concat_axis=0, tiled=True)
    got = got.reshape(planes, share, rows, width)
    return lax.dynamic_index_in_dim(got, plane_index() // planes, 1, keepdims=False)


def from_below(block, distance):
    planes = lax.axis_size("z")
    return lax.ppermute(block, "z", [(i, i + distance) for i in range(planes - distance)])


def from_above(block, distance):
    planes = lax.axis_size("z")
    return lax.ppermute(block, "z", [(i + distance, i) for i in range(planes - distance)])


def gather_z(piece):
    return lax.all_gather(piece, "z", axis=0, tiled=False)


def scatter_z(terms):
    return lax.psum_scatter(terms.astype(BF), "z", scatter_dimension=0, tiled=False)


def tile_masks(meta, key_tile, query_tile):
    key_first = meta[2 + key_tile]
    key_last = key_first + (TILE - 1)
    query_first = meta[6 + query_tile]
    query_last = query_first + (TILE - 1)
    start_first = meta[10 + query_tile]
    start_last = meta[14 + query_tile]
    some = (key_last >= start_first) & (key_first <= query_last)
    whole = (key_first >= start_last) & (key_last <= query_first)
    return some, whole


def key_positions(meta, key_tile, count, width):
    row = lax.broadcasted_iota(jnp.int32, (TILE, width), 0) ^ meta[1]
    parts = [meta[2 + key_tile + i] + row for i in range(count)]
    return jnp.concatenate(parts, 0) if count > 1 else parts[0]


def visit_tiles(meta, tiles, work):
    def query_step(q, _):
        needed, whole = jnp.int32(0), jnp.int32(0)
        for k in range(tiles):
            some, all_ = tile_masks(meta, k, q)
            needed += some.astype(jnp.int32)
            whole += all_.astype(jnp.int32)
        strip = needed >= tiles - 1
        pl.when(whole == tiles)(lambda: work(q, 0, tiles, False))
        pl.when(strip & (whole < tiles))(lambda: work(q, 0, tiles, True))

        @pl.when(jnp.logical_not(strip) & (needed > 0))
        def _():
            def key_step(k, _):
                some, all_ = tile_masks(meta, k, q)
                pl.when(some & all_)(lambda: work(q, k, 1, False))
                pl.when(some & jnp.logical_not(all_))(lambda: work(q, k, 1, True))
                return 0

            lax.fori_loop(0, tiles, key_step, 0)

        return 0

    lax.fori_loop(0, tiles, query_step, 0)


def beside(ref, parts, rows, columns):
    return jnp.concatenate([ref[i * rows : (i + 1) * rows, columns] for i in range(parts)], 1)


def forward_kernel(meta, pair, query, rows, acc_in, total_in, acc, total, keys):
    head = pair.shape[0] // 2
    heads = query.shape[0] // head
    tiles = pair.shape[1] // TILE
    acc[...] = acc_in[...]
    total[...] = total_in[...]

    @pl.when(meta[0] > 0)
    def _():
        keys[...] = pair[:head, :].astype(F32).T.astype(BF)

        def work(q, k, count, masked):
            columns = pl.ds(pl.multiple_of(q * TILE, TILE), TILE)
            span = pl.ds(pl.multiple_of(k * TILE, TILE), count * TILE)
            scores = dot(keys[span, :], beside(query, heads, head, columns), 1, 0)
            terms = jnp.exp2(scores * LOG2E)
            if masked:
                key_pos = key_positions(meta, k, count, terms.shape[1])
                last = jnp.concatenate([rows[0:1, columns]] * heads, 1)
                first = jnp.concatenate([rows[1:2, columns]] * heads, 1)
                terms = jnp.where((key_pos <= last) & (key_pos >= first), terms, 0.0)
            sums = jnp.sum(terms, 0, keepdims=True)
            values = dot(pair[head:, span], terms.astype(BF), 1, 0)
            for h in range(heads):
                here = slice(h * TILE, (h + 1) * TILE)
                total[h : h + 1, columns] += sums[:, here]
                acc[h * head : (h + 1) * head, columns] += values[:, here]

        visit_tiles(meta, tiles, work)


def attend(meta, pair, query, rows, acc, total):
    head = pair.shape[0] // 2
    count = pair.shape[1]
    vmem = pl.BlockSpec(memory_space=pltpu.VMEM)
    return pl.pallas_call(
        forward_kernel,
        out_shape=(
            jax.ShapeDtypeStruct(acc.shape, F32),
            jax.ShapeDtypeStruct(total.shape, F32),
        ),
        in_specs=[pl.BlockSpec(memory_space=pltpu.SMEM)] + [vmem] * 5,
        out_specs=(vmem, vmem),
        scratch_shapes=[pltpu.VMEM((count, head), BF)],
        compiler_params=pltpu.CompilerParams(vmem_limit_bytes=32 * 1024 * 1024),
        cost_estimate=pl.CostEstimate(flops=0, bytes_accessed=pair.size, transcendentals=0),
    )(meta, pair, query, rows, acc, total)


def backward_kernel(
    meta,
    pair,
    query,
    out_grad,
    rows,
    log_total,
    delta,
    query_in,
    query_grad,
    pair_out,
    keys,
    values,
    pair_grad,
):
    head = pair.shape[0] // 2
    heads = query.shape[0] // head
    tiles = pair.shape[1] // TILE
    query_grad[...] = query_in[...]
    pair_grad[...] = jnp.zeros(pair_grad.shape, F32)

    @pl.when(meta[0] > 0)
    def _():
        keys[...] = pair[:head, :].astype(F32).T.astype(BF)
        values[...] = pair[head:, :].astype(F32).T.astype(BF)

        def work(q, k, count, masked):
            columns = pl.ds(pl.multiple_of(q * TILE, TILE), TILE)
            span = pl.ds(pl.multiple_of(k * TILE, TILE), count * TILE)
            queries = beside(query, heads, head, columns)
            outs = beside(out_grad, heads, head, columns)
            scores = dot(keys[span, :], queries, 1, 0)
            weights = jnp.exp2(scores * LOG2E - beside(log_total, heads, 1, columns))
            if masked:
                key_pos = key_positions(meta, k, count, weights.shape[1])
                last = jnp.concatenate([rows[0:1, columns]] * heads, 1)
                first = jnp.concatenate([rows[1:2, columns]] * heads, 1)
                weights = jnp.where((key_pos <= last) & (key_pos >= first), weights, 0.0)
            weight_grad = dot(values[span, :], outs, 1, 0)
            score_grad = (weights * (weight_grad - beside(delta, heads, 1, columns))).astype(BF)
            pair_grad[:head, span] += dot(queries, score_grad, 1, 1)
            pair_grad[head:, span] += dot(outs, weights.astype(BF), 1, 1)
            more = dot(pair[:head, span], score_grad, 1, 0)
            for h in range(heads):
                query_grad[h * head : (h + 1) * head, columns] += more[
                    :, h * TILE : (h + 1) * TILE
                ]

        visit_tiles(meta, tiles, work)

    pair_out[...] = pair_grad[...].astype(pair_out.dtype)


def attend_back(meta, pair, query, out_grad, rows, log_total, delta, query_grad, dtype):
    head = pair.shape[0] // 2
    count = pair.shape[1]
    vmem = pl.BlockSpec(memory_space=pltpu.VMEM)
    return pl.pallas_call(
        backward_kernel,
        out_shape=(
            jax.ShapeDtypeStruct(query_grad.shape, F32),
            jax.ShapeDtypeStruct(pair.shape, dtype),
        ),
        in_specs=[pl.BlockSpec(memory_space=pltpu.SMEM)] + [vmem] * 7,
        out_specs=(vmem, vmem),
        scratch_shapes=[
            pltpu.VMEM((count, head), BF),
            pltpu.VMEM((count, head), BF),
            pltpu.VMEM(pair.shape, F32),
        ],
        compiler_params=pltpu.CompilerParams(vmem_limit_bytes=32 * 1024 * 1024),
        cost_estimate=pl.CostEstimate(
            flops=10 * count * query.size,
            bytes_accessed=2 * (pair.size + 2 * query.size) + 8 * query.size,
            transcendentals=count * query.size // head,
        ),
    )(meta, pair, query, out_grad, rows, log_total, delta, query_grad)


def ffn_weights(packed, unit):
    whole = gather_z(packed)
    width = whole.shape[-1]
    return (
        whole[:, : 2 * unit].reshape(-1, width),
        whole[:, 2 * unit : 3 * unit].reshape(-1, width),
        whole[:, 3 * unit :],
    )


def ffn_up(normed, both, planes):
    hidden = dot(both, normed, 1, 1)
    hidden = hidden.reshape(planes, 2, -1, hidden.shape[-1])
    gate, up = hidden[:, 0], hidden[:, 1]
    act = (jax.nn.silu(gate) * up).astype(BF)
    return gate, up, act.reshape(-1, act.shape[-1])


def ffn_back(act_grad, gate, up, normed, both):
    act_grad = act_grad.reshape(gate.shape)
    sig = jax.nn.sigmoid(gate)
    gate_grad = (act_grad * up * sig * (1.0 + gate * (1.0 - sig))).astype(BF)
    up_grad = (act_grad * gate * sig).astype(BF)
    hidden_grad = jnp.stack([gate_grad, up_grad], 1).reshape(-1, gate.shape[-1])
    return hidden_grad, dot(hidden_grad, both, 0, 0)


def by_plane(grad, planes):
    return grad.astype(BF).reshape(planes, -1, grad.shape[-1])


def ffn_shards(both, down):
    return unpack(both) + (down.astype(F32),)


def body(
    tokens,
    doc_starts,
    conv_norm,
    conv_in,
    conv_kernel,
    conv_out,
    ffn1_norm,
    ffn1_gate,
    ffn1_up_weight,
    ffn1_down,
    attn_norm,
    attn_query,
    attn_key,
    attn_value,
    qk_gains,
    attn_output,
    ffn2_norm,
    ffn2_gate,
    ffn2_up_weight,
    ffn2_down,
    cotangent,
):
    planes = lax.axis_size("z")
    z = lax.axis_index("z")
    own = plane_index()
    rows, width = tokens.shape
    count = 8 * rows
    owned = conv_norm.shape[0]
    head = qk_gains.shape[1]
    heads = attn_query.shape[1] // (8 * head)
    part = width // 8
    devices = 8 * planes

    places = own ^ jnp.arange(8, dtype=jnp.int32)
    positions = z * count + places[:, None] * rows + jnp.arange(rows, dtype=jnp.int32)[None, :]
    positions = positions.reshape(-1)
    starts = jnp.max(
        jnp.where(doc_starts[None, :] <= positions[:, None], doc_starts[None, :], 0), 1
    )
    keep_one = (positions - 1 >= starts).astype(F32).reshape(8, rows, 1)
    keep_two = (positions - 2 >= starts).astype(F32).reshape(8, rows, 1)

    small = jnp.stack([conv_norm, ffn1_norm, attn_norm, ffn2_norm], 1)
    small = jnp.concatenate([small, conv_kernel, jnp.zeros((owned, 121), BF)], 1)
    columns = spread(conv_in, small, devices)
    columns, tokens = lax.optimization_barrier((columns, tokens))
    columns = swap_all(columns).reshape(width, -1)
    unit = ffn1_down.shape[0]
    query_columns = jnp.concatenate(
        [
            attn_query.reshape(owned, 8, -1).transpose(1, 0, 2),
            attn_key.reshape(owned, 8, -1).transpose(1, 0, 2),
            attn_value.reshape(owned, 8, -1).transpose(1, 0, 2),
        ],
        2,
    )
    columns, query_columns = lax.optimization_barrier((columns, query_columns))
    query_columns = lax.all_to_all(query_columns, PLANE, split_axis=0, concat_axis=0, tiled=True)
    query_columns = query_columns.reshape(8 * owned, -1)
    fold = width // query_columns.shape[1]
    packed_two = pack(
        ffn2_gate, ffn2_up_weight, ffn2_down, jnp.concatenate(jnp.split(query_columns, fold), 1)
    )
    conv_weight = columns[:, : 3 * part]
    small = columns[:, 3 * part : 3 * part + 8].T.astype(F32)
    conv_gain, ffn1_gain, attn_gain, ffn2_gain = (small[i : i + 1] for i in range(4))
    taps = lax.dynamic_slice(small[4:7], (0, own * part), (3, part))[:, None, None, :]

    edge = from_below(tokens[rows - 16 :], 1)
    piece = jnp.concatenate([tokens, edge], 0)
    chips = [piece] + [chip_swap(piece, d) for d in (1, 2, 3)]
    chips[1], ffn1_gate = lax.optimization_barrier((chips[1], ffn1_gate))
    tokens_all, edges = gather_cores(chips, (rows, 16))
    below = lax.dynamic_slice(edges, ((own ^ 7) * 16, 0), (16, width)).astype(F32)
    packed_one = pack(ffn1_gate, ffn1_up_weight, ffn1_down)
    packed_one, conv_out = lax.optimization_barrier((packed_one, conv_out))
    both_one, down_one, _ = ffn_weights(packed_one, unit)
    row_pieces = rows_of_plane_index(conv_out, attn_output)
    raw = tokens_all.astype(F32)

    residual = tokens.astype(F32)
    normed_conv, raw_inverse = rms_forward(raw, conv_gain)
    normed_conv = normed_conv.astype(BF)
    projected = dot(normed_conv, conv_weight, 1, 0).reshape(8, rows, 3 * part)
    in_gate = projected[..., :part]
    out_gate = projected[..., part : 2 * part]
    conv_values = projected[..., 2 * part :]
    gated = in_gate * conv_values
    def pick(table, wanted):
        chosen = (places[None, :] == wanted[:, None]).astype(F32)
        return jnp.sum(chosen[:, :, None, None] * table[None], 1)

    tails = gated[:, rows - 2 :]
    normed_below, _ = rms_forward(below, conv_gain)
    rim = dot(normed_below.astype(BF), conv_weight, 1, 0)[14:]
    rim = (rim[:, :part] * rim[:, 2 * part :])[None]
    before = pick(tails, places - 1) + jnp.where(places == 0, 1.0, 0.0)[:, None, None] * rim
    prev_one = jnp.concatenate([before[:, 1:], gated[:, :-1]], 1) * keep_one
    prev_two = jnp.concatenate([before, gated[:, :-2]], 1) * keep_two
    conv_sum = taps[2] * gated + taps[1] * prev_one + taps[0] * prev_two
    mixed = (out_gate * conv_sum).astype(BF)
    mixed = mixed.reshape(count, part)
    mixed, row_pieces = lax.optimization_barrier((mixed, row_pieces))
    conv_out_rows, attn_output_rows = place(row_pieces, owned)
    hidden_one = residual + scatter_plane(dot(mixed, conv_out_rows, 1, 0))

    both_two, down_two, qkv_weight = ffn_weights(packed_two, unit)
    qkv_weight = jnp.concatenate(jnp.split(qkv_weight, fold, 2), 1).reshape(width, -1)

    normed, inverse_one = rms_forward(hidden_one, ffn1_gain)
    normed_one = gather_plane(normed.astype(BF))
    gate_one, up_one, act_one = ffn_up(normed_one, both_one, planes)
    hidden_two = hidden_one + scatter_plane(dot(act_one, down_one, 0, 0))

    normed, inverse_attn = rms_forward(hidden_two, attn_gain)
    normed_attn = gather_plane(normed.astype(BF))
    normed_attn, cotangent_low = lax.optimization_barrier((normed_attn, cotangent))
    cotangent_all = gather_plane(cotangent_low)
    raw_qkv = dot(qkv_weight, normed_attn, 0, 1)
    query_raw = raw_qkv[: heads * head].reshape(heads, head, count)
    key_raw = raw_qkv[heads * head : (heads + 1) * head][None]
    value_low = raw_qkv[(heads + 1) * head :].astype(BF)
    gains = qk_gains.astype(F32)
    query_gain, key_gain = gains[0][None, :, None], gains[1][None, :, None]
    half = head // 2
    frequency = jnp.power(
        jnp.float32(ROPE_BASE), -jnp.arange(half, dtype=F32) * 2.0 / head
    )
    angles = frequency[:, None] * positions.astype(F32)[None, :]
    cosine, sine = jnp.cos(angles)[None], jnp.sin(angles)[None]

    def rope(v):
        first, second = v[:, :half], v[:, half:]
        return jnp.concatenate(
            [first * cosine - second * sine, second * cosine + first * sine], 1
        )

    def rope_back(g):
        first, second = g[:, :half], g[:, half:]
        return jnp.concatenate(
            [first * cosine + second * sine, second * cosine - first * sine], 1
        )

    query_unit, query_inverse = rms_forward(query_raw, query_gain, 1)
    key_unit, key_inverse = rms_forward(key_raw, key_gain, 1)
    query_low = rope(query_unit).astype(BF)
    key_low = rope(key_unit).astype(BF)[0]

    tiles = count // TILE

    query_rows = (query_low.astype(F32) * (head**-0.5)).astype(BF).reshape(heads * head, count)
    row_info = jnp.stack([positions, starts])
    tile_first = (own // 2 ^ jnp.arange(tiles, dtype=jnp.int32)) * TILE
    core = own % 2 * rows
    tile_starts = jnp.max(
        jnp.where(
            doc_starts[None, :]
            <= (z * count + tile_first[:, None, None] + jnp.array([[0], [TILE - 1]])),
            doc_starts[None, None, :],
            0,
        ),
        2,
    )

    def meta_of(step):
        return jnp.concatenate(
            [
                jnp.stack([(z >= step).astype(jnp.int32), core]),
                (z - step) * count + tile_first,
                z * count + tile_first,
                tile_starts[:, 0],
                tile_starts[:, 1],
            ]
        ).astype(jnp.int32)

    metas = [meta_of(step) for step in range(planes)]
    pair = jnp.concatenate([key_low, value_low], 0)
    pair, both_two, down_two = lax.optimization_barrier((pair, both_two, down_two))
    pairs = [pair] + [from_below(pair, step) for step in range(1, planes)]
    acc = jnp.zeros((heads * head, count), F32)
    total = jnp.zeros((heads, count), F32)
    for step in range(planes):
        acc, total = attend(metas[step], pairs[step], query_rows, row_info, acc, total)
    log_total = jnp.log2(total)
    mixed_heads = acc.reshape(heads, head, count) / total[:, None, :]
    head_low = mixed_heads.astype(BF).reshape(heads * head, count)
    hidden_three = hidden_two + scatter_plane(dot(head_low, attn_output_rows, 0, 0))

    normed, inverse_two = rms_forward(hidden_three, ffn2_gain)
    normed_two = gather_plane(normed.astype(BF))
    act_grad_two = dot(down_two, cotangent_all, 1, 1)
    gate_two, up_two, act_two = ffn_up(normed_two, both_two, planes)
    hidden_grad, partial = ffn_back(act_grad_two, gate_two, up_two, normed_two, both_two)
    normed_grad = scatter_plane(partial)
    down_two_terms = by_plane(dot(act_two, cotangent_all, 1, 0), planes)
    both_two_terms = by_plane(dot(hidden_grad, normed_two, 1, 0), planes)
    normed_grad, both_two_terms, down_two_terms = lax.optimization_barrier(
        (normed_grad, both_two_terms, down_two_terms)
    )
    down_two_sum = scatter_z(down_two_terms)
    residual_grad, gain_rows_two = rms_backward(hidden_three, inverse_two, ffn2_gain, normed_grad)
    gradient = cotangent.astype(F32) + residual_grad
    gradient_low = gather_plane(gradient.astype(BF))
    out_grad = dot(attn_output_rows, gradient_low, 1, 1).astype(BF)
    delta = jnp.sum(out_grad.astype(F32).reshape(mixed_heads.shape) * mixed_heads, 1)
    attn_output_terms = by_plane(dot(head_low, gradient_low, 1, 0), planes)
    attn_output_terms, out_grad = lax.optimization_barrier((attn_output_terms, out_grad))
    attn_output_terms = rows_to_planes(attn_output_terms)

    query_grad = jnp.zeros((heads * head, count), F32)
    arrived = []
    for step in range(planes - 1, -1, -1):
        if len(arrived) > 1:
            query_grad, arrived[-2] = lax.optimization_barrier((query_grad, arrived[-2]))
        if step == 0:
            query_grad, attn_output_terms, down_two_sum = lax.optimization_barrier(
                (query_grad, attn_output_terms, down_two_sum)
            )
        query_grad, pair_grad = attend_back(
            metas[step],
            pairs[step],
            query_rows,
            out_grad,
            row_info,
            log_total,
            delta,
            query_grad,
            BF if step > 0 else F32,
        )
        if step > 0:
            arrived.append(from_above(pair_grad, step))
    for block in arrived:
        pair_grad = pair_grad + block.astype(F32)
    terms_two = jnp.concatenate([both_two_terms, attn_output_terms], 1)
    pair_grad, terms_two = lax.optimization_barrier((pair_grad, terms_two))
    sum_two = scatter_z(terms_two)
    query_tok = query_grad.reshape(heads, head, count) * (head**-0.5)
    query_raw_grad, query_gain_rows = rms_backward(
        query_raw, query_inverse, query_gain, rope_back(query_tok), 1
    )
    key_raw_grad, key_gain_rows = rms_backward(
        key_raw, key_inverse, key_gain, rope_back(pair_grad[None, :head]), 1
    )
    qk_rows = jnp.stack(
        [jnp.sum(query_gain_rows, (0, 2)), jnp.sum(key_gain_rows, (0, 2))]
    ).reshape(-1)
    qkv_grad = jnp.concatenate(
        [
            query_raw_grad.reshape(heads * head, count).astype(BF),
            key_raw_grad[0].astype(BF),
            pair_grad[head:].astype(BF),
        ],
        0,
    )
    normed_grad = scatter_plane(dot(qkv_grad, qkv_weight, 0, 1))
    residual_grad, gain_rows_attn = rms_backward(hidden_two, inverse_attn, attn_gain, normed_grad)
    gradient = gradient + residual_grad
    qkv_weight_grad = dot(normed_attn, qkv_grad, 0, 1)

    qkv_terms = by_plane(qkv_weight_grad, planes)
    qkv_terms = jnp.concatenate(jnp.split(qkv_terms, fold, 1), 2)

    gradient_low = gather_plane(gradient.astype(BF))
    down_one_terms = by_plane(dot(act_one, gradient_low, 1, 0), planes)
    act_grad_one = dot(down_one, gradient_low, 1, 1)
    hidden_grad, partial = ffn_back(act_grad_one, gate_one, up_one, normed_one, both_one)
    down_one_terms = jnp.concatenate([down_one_terms, qkv_terms], 1)
    partial, down_one_terms = lax.optimization_barrier((partial, down_one_terms))
    down_one_sum = scatter_z(down_one_terms)
    normed_grad = scatter_plane(partial)
    both_one_terms = by_plane(dot(hidden_grad, normed_one, 1, 0), planes)
    normed_grad, both_one_terms, sum_two = lax.optimization_barrier(
        (normed_grad, both_one_terms, sum_two)
    )
    grad_ffn2 = ffn_shards(sum_two[: 2 * unit], down_two_sum)
    grad_attn_output = sum_two[2 * unit :].astype(F32)
    residual_grad, gain_rows_one = rms_backward(hidden_one, inverse_one, ffn1_gain, normed_grad)
    gradient = gradient + residual_grad

    gradient_low = gather_plane(gradient.astype(BF))
    mixed_grad = dot(gradient_low, conv_out_rows, 1, 1).reshape(8, rows, part)
    conv_out_terms = rows_to_planes(by_plane(dot(mixed, gradient_low, 0, 0), planes))
    terms_one = jnp.concatenate([both_one_terms, conv_out_terms], 1)
    mixed_grad, terms_one = lax.optimization_barrier((mixed_grad, terms_one))
    sum_one = scatter_z(terms_one)
    out_gate_grad = mixed_grad * conv_sum
    conv_grad = mixed_grad * out_gate
    kernel_grad = jnp.stack(
        [
            jnp.sum(conv_grad * prev_two, (0, 1)),
            jnp.sum(conv_grad * prev_one, (0, 1)),
            jnp.sum(conv_grad * gated, (0, 1)),
        ],
        1,
    )
    back_one = taps[1] * conv_grad * keep_one
    back_two = taps[0] * conv_grad * keep_two
    fronts = jnp.concatenate([back_one[:, :1], back_two[:, :2]], 1)
    rim = lax.ppermute(
        pick(fronts, jnp.full((1,), 0)), "z", [(i + 1, i) for i in range(planes - 1)]
    )
    after = pick(fronts, places + 1) + jnp.where(places == 7, 1.0, 0.0)[:, None, None] * rim
    gated_grad = (
        taps[2] * conv_grad
        + jnp.concatenate([back_one[:, 1:], after[:, :1]], 1)
        + jnp.concatenate([back_two[:, 2:], after[:, 1:]], 1)
    )
    projected_grad = (
        jnp.concatenate([gated_grad * conv_values, out_gate_grad, gated_grad * in_gate], 2)
        .astype(BF)
        .reshape(count, 3 * part)
    )
    partial = dot(projected_grad, conv_weight, 1, 1)
    gain_conv = jnp.sum(partial * (raw * raw_inverse), 0)
    conv_in_terms = dot(normed_conv, projected_grad, 0, 0).astype(BF)
    normed_grad = scatter_plane(partial)
    normed_grad, conv_in_terms, down_one_sum = lax.optimization_barrier(
        (normed_grad, conv_in_terms, down_one_sum)
    )
    grad_ffn1 = ffn_shards(sum_one[: 2 * unit], down_one_sum[:unit])
    grad_conv_out = sum_one[2 * unit :].astype(F32)
    qkv_sum = jnp.concatenate(jnp.split(down_one_sum[unit:], fold, 1), 0)
    query_part = heads * head
    blocks = lax.all_to_all(
        qkv_sum.reshape(8, owned, -1), PLANE, split_axis=0, concat_axis=0, tiled=True
    )
    grad_query, grad_key, grad_value = lanes_back(
        blocks,
        (8 * query_part, 8 * head, 8 * head),
        lambda j, outs: (
            (0, query_part, outs[0], j * query_part),
            (query_part, head, outs[1], j * head),
            (query_part + head, head, outs[2], j * head),
        ),
    )
    blocks = swap_all(conv_in_terms.reshape(devices, owned, -1))
    (grad_conv_in,) = lanes_back(
        blocks,
        (3 * width,),
        lambda j, outs: tuple(
            (i * part, part, outs[0], (i * 8 + j) * part) for i in range(3)
        ),
    )
    inverse = lax.rsqrt(jnp.mean(residual * residual, axis=-1, keepdims=True) + EPSILON)
    act_two, normed_grad = lax.optimization_barrier((act_two, normed_grad))
    output = (hidden_three + scatter_plane(dot(act_two, down_two, 0, 0))).astype(BF)
    residual_grad, _ = rms_backward(residual, inverse, conv_gain, normed_grad)
    grad_tokens = gradient + residual_grad
    kernel_all = lax.dynamic_update_slice(jnp.zeros((width, 3), F32), kernel_grad, (own * part, 0))
    small_grads = jnp.concatenate(
        [
            gain_conv.reshape(devices, owned),
            jnp.sum(gain_rows_one, 0).reshape(devices, owned),
            jnp.sum(gain_rows_attn, 0).reshape(devices, owned),
            jnp.sum(gain_rows_two, 0).reshape(devices, owned),
            kernel_all.reshape(devices, 3 * owned),
            jnp.broadcast_to(qk_rows[None], (devices, qk_rows.shape[0])),
        ],
        1,
    )
    small_grads = lax.all_to_all(
        small_grads[:, None, :], EVERY, split_axis=0, concat_axis=0, tiled=True
    )
    small_grads = jnp.sum(small_grads, (0, 1))
    grad_norms = [small_grads[i * owned : (i + 1) * owned] for i in range(4)]
    grad_kernel = small_grads[4 * owned : 7 * owned].reshape(owned, 3)
    grad_gains = small_grads[7 * owned :].reshape(2, head)

    return (
        output,
        grad_tokens,
        grad_norms[0],
        grad_conv_in,
        grad_kernel,
        grad_conv_out,
        grad_norms[1],
        grad_ffn1[0],
        grad_ffn1[1],
        grad_ffn1[2],
        grad_norms[2],
        grad_query,
        grad_key,
        grad_value,
        grad_gains,
        grad_attn_output,
        grad_norms[3],
        grad_ffn2[0],
        grad_ffn2[1],
        grad_ffn2[2],
    )


def solution(mesh):
    seq, heads = mesh.shape["seq"], mesh.shape["head"]
    grid = Mesh(mesh.devices.reshape(seq // 2, 2, heads // 2, 2), EVERY)
    lead, both, last = P(EVERY), P(EVERY, None), P(None, EVERY)
    return jax.shard_map(
        body,
        mesh=grid,
        in_specs=(
            both,
            P(),
            lead,
            both,
            both,
            both,
            lead,
            last,
            last,
            both,
            lead,
            both,
            both,
            both,
            P(),
            both,
            lead,
            last,
            last,
            both,
            both,
        ),
        out_specs=(
            both,
            both,
            lead,
            both,
            both,
            both,
            lead,
            last,
            last,
            both,
            lead,
            both,
            both,
            both,
            P(),
            both,
            lead,
            last,
            last,
            both,
        ),
        check_vma=False,
    )
```

```python
import functools

import jax
import jax.numpy as jnp
from jax import lax
from jax.experimental import pallas as pl
from jax.experimental.pallas import tpu as pltpu
from jax.sharding import Mesh
from jax.sharding import PartitionSpec as P

EPSILON = 1e-05
ROPE_BASE = 1000000.0
LOG2E = 1.4426950408889634
BF = jnp.bfloat16
F32 = jnp.float32
PLANE = ("x", "y", "c")
EVERY = ("z", "x", "y", "c")
TILE = 256


def dot(left, right, left_dim, right_dim):
    return lax.dot_general(
        left, right, (((left_dim,), (right_dim,)), ((), ())), preferred_element_type=F32
    )


def rms_forward(values, gain, axis=-1):
    inverse = lax.rsqrt(jnp.mean(values * values, axis=axis, keepdims=True) + EPSILON)
    return values * inverse * gain, inverse


def rms_backward(values, inverse, gain, gradient, axis=-1):
    unit = values * inverse
    scaled = gradient * gain
    result = inverse * (scaled - unit * jnp.mean(scaled * unit, axis=axis, keepdims=True))
    return result, gradient * unit


def plane_index():
    return lax.axis_index(PLANE)


def swap_all(blocks):
    return lax.all_to_all(blocks, EVERY, split_axis=0, concat_axis=0, tiled=True)


SWAP = [(0, 1), (1, 0)]


def core_swap(block):
    return lax.ppermute(block, "c", SWAP)


def chip_swap(block, distance):
    return lax.ppermute(block, ("x", "y"), [(i, i ^ distance) for i in range(4)])


def join_kernel(take, *refs):
    pieces, outs = refs[: -len(take)], refs[-len(take) :]
    first = 0
    for rows, out in zip(take, outs):
        for i, piece in enumerate(pieces):
            out[i * rows : (i + 1) * rows, :] = piece[first : first + rows, :]
        first += rows


def join(pieces, take=None):
    rows, width = pieces[0].shape
    take = take or (rows,)
    vmem = pl.BlockSpec(memory_space=pltpu.VMEM)
    out = pl.pallas_call(
        functools.partial(join_kernel, take),
        out_shape=tuple(
            jax.ShapeDtypeStruct((len(pieces) * t, width), pieces[0].dtype) for t in take
        ),
        in_specs=[vmem] * len(pieces),
        out_specs=(vmem,) * len(take),
        compiler_params=pltpu.CompilerParams(vmem_limit_bytes=16 * 1024 * 1024),
        cost_estimate=pl.CostEstimate(
            flops=0, bytes_accessed=4 * len(pieces) * rows * width, transcendentals=0
        ),
    )(*pieces)
    return out if len(take) > 1 else out[0]


def pack_kernel(*refs):
    gate, up, out = refs[0], refs[1], refs[-1]
    unit = gate.shape[1]
    out[:unit, :] = gate[...].astype(F32).T.astype(BF)
    out[unit : 2 * unit, :] = up[...].astype(F32).T.astype(BF)
    if len(refs) > 3:
        out[2 * unit :, :] = refs[2][...]


def pack(gate, up, *down):
    width, unit = gate.shape
    if unit % 16:
        return jnp.concatenate([gate.T, up.T, *down], 0)
    vmem = pl.BlockSpec(memory_space=pltpu.VMEM)
    rows = (2 + len(down)) * unit
    return pl.pallas_call(
        pack_kernel,
        out_shape=jax.ShapeDtypeStruct((rows, width), BF),
        in_specs=[vmem] * (2 + len(down)),
        out_specs=vmem,
        compiler_params=pltpu.CompilerParams(vmem_limit_bytes=16 * 1024 * 1024),
        cost_estimate=pl.CostEstimate(flops=0, bytes_accessed=4 * rows * width, transcendentals=0),
    )(gate, up, *down)


def unpack_kernel(both, gate, up):
    unit = both.shape[0] // 2
    gate[...] = both[:unit, :].astype(F32).T
    up[...] = both[unit:, :].astype(F32).T


def unpack(both):
    unit, width = both.shape[0] // 2, both.shape[1]
    if unit % 16:
        both = both.astype(F32)
        return both[:unit].T, both[unit:].T
    vmem = pl.BlockSpec(memory_space=pltpu.VMEM)
    out = jax.ShapeDtypeStruct((width, unit), F32)
    return pl.pallas_call(
        unpack_kernel,
        out_shape=(out, out),
        in_specs=[vmem],
        out_specs=(vmem, vmem),
        compiler_params=pltpu.CompilerParams(vmem_limit_bytes=16 * 1024 * 1024),
        cost_estimate=pl.CostEstimate(
            flops=0, bytes_accessed=12 * unit * width, transcendentals=0
        ),
    )(both)


def lanes_kernel(splits, blocks, *outs):
    planes = blocks.shape[0] // 8
    for j in range(8):
        block = blocks[j].astype(F32)
        for k in range(1, planes):
            block = block + blocks[8 * k + j].astype(F32)
        for first, size, out, place in splits(j, outs):
            out[:, place : place + size] = block[:, first : first + size]


def lanes_back(blocks, widths, splits):
    vmem = pl.BlockSpec(memory_space=pltpu.VMEM)
    rows = blocks.shape[1]
    return pl.pallas_call(
        functools.partial(lanes_kernel, splits),
        out_shape=tuple(jax.ShapeDtypeStruct((rows, w), F32) for w in widths),
        in_specs=[vmem],
        out_specs=(vmem,) * len(widths),
        compiler_params=pltpu.CompilerParams(vmem_limit_bytes=16 * 1024 * 1024),
        cost_estimate=pl.CostEstimate(
            flops=0, bytes_accessed=4 * blocks.size, transcendentals=0
        ),
    )(blocks)


def spread_kernel(weight, small, out):
    part = weight.shape[1] // 24
    for j in range(8):
        for i in range(3):
            first = (i * 8 + j) * part
            out[j, :, i * part : (i + 1) * part] = weight[:, first : first + part]
        out[j, :, 3 * part :] = small[...]
    for k in range(8, out.shape[0]):
        out[k] = out[k % 8]


def spread(weight, small, devices):
    rows = weight.shape[0]
    width = weight.shape[1] // 8 + small.shape[1]
    if rows % 16:
        columns = jnp.concatenate(
            [
                weight.reshape(rows, 3, 8, -1).transpose(2, 0, 1, 3).reshape(8, rows, -1),
                jnp.broadcast_to(small[None], (8,) + small.shape),
            ],
            2,
        )
        return jnp.tile(columns, (devices // 8, 1, 1))
    vmem = pl.BlockSpec(memory_space=pltpu.VMEM)
    return pl.pallas_call(
        spread_kernel,
        out_shape=jax.ShapeDtypeStruct((devices, rows, width), BF),
        in_specs=[vmem] * 2,
        out_specs=vmem,
        compiler_params=pltpu.CompilerParams(vmem_limit_bytes=16 * 1024 * 1024),
        cost_estimate=pl.CostEstimate(
            flops=0, bytes_accessed=4 * devices * rows * width, transcendentals=0
        ),
    )(weight, small)


def gather_plane(piece):
    return gather_cores([piece] + [chip_swap(piece, d) for d in (1, 2, 3)])


def gather_cores(chips, take=None):
    return join([v for chip in chips for v in (chip, core_swap(chip))], take)


def place_kernel(cut, z, *refs):
    planes = len(refs) - 2
    pieces, first, second = refs[:planes], refs[-2], refs[-1]
    rest = pieces[0].shape[0] - cut
    for t, piece in enumerate(pieces):
        k = (z[0] - t + planes) % planes
        first[pl.ds(pl.multiple_of(k * cut, cut), cut), :] = piece[:cut, :]
        second[pl.ds(pl.multiple_of(k * rest, rest), rest), :] = piece[cut:, :]


def place(pieces, cut):
    planes = len(pieces)
    rows, width = pieces[0].shape
    z = lax.axis_index("z")
    if cut % 16 or rows % 16:
        stack = jnp.stack(pieces)
        order = [
            lax.dynamic_index_in_dim(stack, (z - k) % planes, 0, keepdims=False)
            for k in range(planes)
        ]
        return (
            jnp.concatenate([v[:cut] for v in order], 0),
            jnp.concatenate([v[cut:] for v in order], 0),
        )
    vmem = pl.BlockSpec(memory_space=pltpu.VMEM)
    return pl.pallas_call(
        functools.partial(place_kernel, cut),
        out_shape=(
            jax.ShapeDtypeStruct((planes * cut, width), BF),
            jax.ShapeDtypeStruct((planes * (rows - cut), width), BF),
        ),
        in_specs=[pl.BlockSpec(memory_space=pltpu.SMEM)] + [vmem] * planes,
        out_specs=(vmem, vmem),
        compiler_params=pltpu.CompilerParams(vmem_limit_bytes=16 * 1024 * 1024),
        cost_estimate=pl.CostEstimate(
            flops=0, bytes_accessed=4 * planes * rows * width, transcendentals=0
        ),
    )(z.reshape(1).astype(jnp.int32), *pieces)


def scatter_plane(parts, *later):
    low = parts.astype(BF).reshape(4, 2, parts.shape[0] // 8, parts.shape[1])
    other = core_swap(low[:, 1])
    mine = [low[d, 0].astype(F32) + other[d].astype(F32) for d in range(4)]
    sent = tuple(mine[d].astype(BF) for d in (3, 1, 2))
    if later:
        sent, later = lax.optimization_barrier((sent, later))
    total = mine[0]
    for d, block in zip((3, 1, 2), sent):
        total = total + chip_swap(block, d).astype(F32)
    return (total, later) if later else total


def rows_of_plane_index(first, second):
    planes = lax.axis_size("z")
    piece = jnp.concatenate([first, second], 0)
    got = []
    for t in range(planes):
        pairs = [
            (j * planes + k, (k + t) % planes * 8 + j) for j in range(8) for k in range(planes)
        ]
        got.append(lax.ppermute(piece, EVERY, pairs))
    return got


def row_block_to_owner(block):
    planes = lax.axis_size("z")
    pairs = [(i * 8 + j, j * planes + i) for j in range(8) for i in range(planes)]
    return lax.ppermute(block, EVERY, pairs)


def from_below(block, distance):
    planes = lax.axis_size("z")
    return lax.ppermute(block, "z", [(i, i + distance) for i in range(planes - distance)])


def from_above(block, distance):
    planes = lax.axis_size("z")
    return lax.ppermute(block, "z", [(i + distance, i) for i in range(planes - distance)])


def gather_z(piece):
    return lax.all_gather(piece, "z", axis=0, tiled=True)


def scatter_z(terms):
    return lax.psum_scatter(terms.astype(BF), "z", scatter_dimension=0, tiled=False)


def tile_masks(meta, key_tile, query_tile):
    key_first = meta[2 + key_tile]
    key_last = key_first + (TILE - 1)
    query_first = meta[6 + query_tile]
    query_last = query_first + (TILE - 1)
    start_first = meta[10 + query_tile]
    start_last = meta[14 + query_tile]
    some = (key_last >= start_first) & (key_first <= query_last)
    whole = (key_first >= start_last) & (key_last <= query_first)
    return some, whole


def key_positions(meta, key_tile, count, width):
    row = lax.broadcasted_iota(jnp.int32, (TILE, width), 0) ^ meta[1]
    parts = [meta[2 + key_tile + i] + row for i in range(count)]
    return jnp.concatenate(parts, 0) if count > 1 else parts[0]


def visit_tiles(meta, tiles, work):
    def query_step(q, _):
        needed, whole = jnp.int32(0), jnp.int32(0)
        for k in range(tiles):
            some, all_ = tile_masks(meta, k, q)
            needed += some.astype(jnp.int32)
            whole += all_.astype(jnp.int32)
        strip = needed >= tiles - 1
        pl.when(whole == tiles)(lambda: work(q, 0, tiles, False))
        pl.when(strip & (whole < tiles))(lambda: work(q, 0, tiles, True))

        @pl.when(jnp.logical_not(strip) & (needed > 0))
        def _():
            def key_step(k, _):
                some, all_ = tile_masks(meta, k, q)
                pl.when(some & all_)(lambda: work(q, k, 1, False))
                pl.when(some & jnp.logical_not(all_))(lambda: work(q, k, 1, True))
                return 0

            lax.fori_loop(0, tiles, key_step, 0)

        return 0

    lax.fori_loop(0, tiles, query_step, 0)


def beside(ref, parts, rows, columns):
    return jnp.concatenate([ref[i * rows : (i + 1) * rows, columns] for i in range(parts)], 1)


def forward_kernel(meta, pair, query, rows, acc_in, total_in, acc, total, keys):
    head = pair.shape[0] // 2
    heads = query.shape[0] // head
    tiles = pair.shape[1] // TILE
    acc[...] = acc_in[...]
    total[...] = total_in[...]

    @pl.when(meta[0] > 0)
    def _():
        keys[...] = pair[:head, :].astype(F32).T.astype(BF)

        def work(q, k, count, masked):
            columns = pl.ds(pl.multiple_of(q * TILE, TILE), TILE)
            span = pl.ds(pl.multiple_of(k * TILE, TILE), count * TILE)
            scores = dot(keys[span, :], beside(query, heads, head, columns), 1, 0)
            terms = jnp.exp2(scores * LOG2E)
            if masked:
                key_pos = key_positions(meta, k, count, terms.shape[1])
                last = jnp.concatenate([rows[0:1, columns]] * heads, 1)
                first = jnp.concatenate([rows[1:2, columns]] * heads, 1)
                terms = jnp.where((key_pos <= last) & (key_pos >= first), terms, 0.0)
            sums = jnp.sum(terms, 0, keepdims=True)
            values = dot(pair[head:, span], terms.astype(BF), 1, 0)
            for h in range(heads):
                here = slice(h * TILE, (h + 1) * TILE)
                total[h : h + 1, columns] += sums[:, here]
                acc[h * head : (h + 1) * head, columns] += values[:, here]

        visit_tiles(meta, tiles, work)


def attend(meta, pair, query, rows, acc, total):
    head = pair.shape[0] // 2
    count = pair.shape[1]
    vmem = pl.BlockSpec(memory_space=pltpu.VMEM)
    return pl.pallas_call(
        forward_kernel,
        out_shape=(
            jax.ShapeDtypeStruct(acc.shape, F32),
            jax.ShapeDtypeStruct(total.shape, F32),
        ),
        in_specs=[pl.BlockSpec(memory_space=pltpu.SMEM)] + [vmem] * 5,
        out_specs=(vmem, vmem),
        scratch_shapes=[pltpu.VMEM((count, head), BF)],
        compiler_params=pltpu.CompilerParams(vmem_limit_bytes=32 * 1024 * 1024),
        cost_estimate=pl.CostEstimate(flops=0, bytes_accessed=pair.size, transcendentals=0),
    )(meta, pair, query, rows, acc, total)


def backward_kernel(
    meta,
    pair,
    query,
    out_grad,
    rows,
    log_total,
    delta,
    query_in,
    query_grad,
    pair_out,
    keys,
    values,
    pair_grad,
):
    head = pair.shape[0] // 2
    heads = query.shape[0] // head
    tiles = pair.shape[1] // TILE
    query_grad[...] = query_in[...]
    pair_grad[...] = jnp.zeros(pair_grad.shape, F32)

    @pl.when(meta[0] > 0)
    def _():
        keys[...] = pair[:head, :].astype(F32).T.astype(BF)
        values[...] = pair[head:, :].astype(F32).T.astype(BF)

        def work(q, k, count, masked):
            columns = pl.ds(pl.multiple_of(q * TILE, TILE), TILE)
            span = pl.ds(pl.multiple_of(k * TILE, TILE), count * TILE)
            queries = beside(query, heads, head, columns)
            outs = beside(out_grad, heads, head, columns)
            scores = dot(keys[span, :], queries, 1, 0)
            weights = jnp.exp2(scores * LOG2E - beside(log_total, heads, 1, columns))
            if masked:
                key_pos = key_positions(meta, k, count, weights.shape[1])
                last = jnp.concatenate([rows[0:1, columns]] * heads, 1)
                first = jnp.concatenate([rows[1:2, columns]] * heads, 1)
                weights = jnp.where((key_pos <= last) & (key_pos >= first), weights, 0.0)
            weight_grad = dot(values[span, :], outs, 1, 0)
            score_grad = (weights * (weight_grad - beside(delta, heads, 1, columns))).astype(BF)
            pair_grad[:head, span] += dot(queries, score_grad, 1, 1)
            pair_grad[head:, span] += dot(outs, weights.astype(BF), 1, 1)
            more = dot(pair[:head, span], score_grad, 1, 0)
            for h in range(heads):
                query_grad[h * head : (h + 1) * head, columns] += more[
                    :, h * TILE : (h + 1) * TILE
                ]

        visit_tiles(meta, tiles, work)

    pair_out[...] = pair_grad[...].astype(pair_out.dtype)


def attend_back(meta, pair, query, out_grad, rows, log_total, delta, query_grad, dtype):
    head = pair.shape[0] // 2
    count = pair.shape[1]
    vmem = pl.BlockSpec(memory_space=pltpu.VMEM)
    return pl.pallas_call(
        backward_kernel,
        out_shape=(
            jax.ShapeDtypeStruct(query_grad.shape, F32),
            jax.ShapeDtypeStruct(pair.shape, dtype),
        ),
        in_specs=[pl.BlockSpec(memory_space=pltpu.SMEM)] + [vmem] * 7,
        out_specs=(vmem, vmem),
        scratch_shapes=[
            pltpu.VMEM((count, head), BF),
            pltpu.VMEM((count, head), BF),
            pltpu.VMEM(pair.shape, F32),
        ],
        compiler_params=pltpu.CompilerParams(vmem_limit_bytes=32 * 1024 * 1024),
        cost_estimate=pl.CostEstimate(
            flops=0, bytes_accessed=pair.size, transcendentals=0
        ),
    )(meta, pair, query, out_grad, rows, log_total, delta, query_grad)


def ffn_up(normed, both, planes):
    hidden = dot(both, normed, 1, 1)
    hidden = hidden.reshape(planes, 2, -1, hidden.shape[-1])
    gate, up = hidden[:, 0], hidden[:, 1]
    act = (jax.nn.silu(gate) * up).astype(BF)
    return gate, up, act.reshape(-1, act.shape[-1])


def ffn_back(act_grad, gate, up, normed, both):
    act_grad = act_grad.reshape(gate.shape)
    sig = jax.nn.sigmoid(gate)
    gate_grad = (act_grad * up * sig * (1.0 + gate * (1.0 - sig))).astype(BF)
    up_grad = (act_grad * gate * sig).astype(BF)
    hidden_grad = jnp.stack([gate_grad, up_grad], 1).reshape(-1, gate.shape[-1])
    return hidden_grad, dot(hidden_grad, both, 0, 0)


def by_plane(grad, planes):
    return grad.astype(BF).reshape(planes, -1, grad.shape[-1])


def ffn_shards(both, down):
    return unpack(both) + (down.astype(F32),)


def body(
    tokens,
    doc_starts,
    conv_norm,
    conv_in,
    conv_kernel,
    conv_out,
    ffn1_norm,
    ffn1_gate,
    ffn1_up_weight,
    ffn1_down,
    attn_norm,
    attn_query,
    attn_key,
    attn_value,
    qk_gains,
    attn_output,
    ffn2_norm,
    ffn2_gate,
    ffn2_up_weight,
    ffn2_down,
    cotangent,
):
    planes = lax.axis_size("z")
    z = lax.axis_index("z")
    own = plane_index()
    rows, width = tokens.shape
    count = 8 * rows
    owned = conv_norm.shape[0]
    head = qk_gains.shape[1]
    heads = attn_query.shape[1] // (8 * head)
    part = width // 8
    devices = 8 * planes

    places = own ^ jnp.arange(8, dtype=jnp.int32)
    positions = z * count + places[:, None] * rows + jnp.arange(rows, dtype=jnp.int32)[None, :]
    positions = positions.reshape(-1)
    starts = jnp.max(
        jnp.where(doc_starts[None, :] <= positions[:, None], doc_starts[None, :], 0), 1
    )
    keep_one = (positions - 1 >= starts).astype(F32).reshape(8, rows, 1)
    keep_two = (positions - 2 >= starts).astype(F32).reshape(8, rows, 1)

    small = jnp.stack([conv_norm, ffn1_norm, attn_norm, ffn2_norm], 1)
    small = jnp.concatenate([small, conv_kernel, jnp.zeros((owned, 121), BF)], 1)
    columns = spread(conv_in, small, devices)
    columns, tokens = lax.optimization_barrier((columns, tokens))
    columns = swap_all(columns).reshape(width, -1)
    unit = ffn1_down.shape[0]
    query_columns = jnp.concatenate(
        [
            attn_query.reshape(owned, 8, -1).transpose(1, 0, 2),
            attn_key.reshape(owned, 8, -1).transpose(1, 0, 2),
            attn_value.reshape(owned, 8, -1).transpose(1, 0, 2),
        ],
        2,
    )
    columns, query_columns = lax.optimization_barrier((columns, query_columns))
    qkv_weight = swap_all(jnp.tile(query_columns, (planes, 1, 1))).reshape(width, -1)
    packed_two = pack(ffn2_gate, ffn2_up_weight)
    conv_weight = columns[:, : 3 * part]
    small = columns[:, 3 * part : 3 * part + 8].T.astype(F32)
    conv_gain, ffn1_gain, attn_gain, ffn2_gain = (small[i : i + 1] for i in range(4))
    taps = lax.dynamic_slice(small[4:7], (0, own * part), (3, part))[:, None, None, :]

    edge = from_below(tokens[rows - 16 :], 1)
    piece = jnp.concatenate([tokens, edge], 0)
    chips = [piece] + [chip_swap(piece, d) for d in (1, 2, 3)]
    chips[1], ffn1_gate = lax.optimization_barrier((chips[1], ffn1_gate))
    packed_one = pack(ffn1_gate, ffn1_up_weight, ffn1_down)
    chips[1], packed_one, conv_out = lax.optimization_barrier((chips[1], packed_one, conv_out))
    tokens_all, edges = gather_cores(chips, (rows, 16))
    below = lax.dynamic_slice(edges, ((own ^ 7) * 16, 0), (16, width)).astype(F32)
    whole_one = gather_z(packed_one)
    row_pieces = rows_of_plane_index(conv_out, attn_output)
    raw = tokens_all.astype(F32)

    residual = tokens.astype(F32)
    normed_conv, raw_inverse = rms_forward(raw, conv_gain)
    normed_conv = normed_conv.astype(BF)
    projected = dot(normed_conv, conv_weight, 1, 0).reshape(8, rows, 3 * part)
    in_gate = projected[..., :part]
    out_gate = projected[..., part : 2 * part]
    conv_values = projected[..., 2 * part :]
    gated = in_gate * conv_values
    def pick(table, wanted):
        chosen = (places[None, :] == wanted[:, None]).astype(F32)
        return jnp.sum(chosen[:, :, None, None] * table[None], 1)

    tails = gated[:, rows - 2 :]
    normed_below, _ = rms_forward(below, conv_gain)
    rim = dot(normed_below.astype(BF), conv_weight, 1, 0)[14:]
    rim = (rim[:, :part] * rim[:, 2 * part :])[None]
    before = pick(tails, places - 1) + jnp.where(places == 0, 1.0, 0.0)[:, None, None] * rim
    prev_one = jnp.concatenate([before[:, 1:], gated[:, :-1]], 1) * keep_one
    prev_two = jnp.concatenate([before, gated[:, :-2]], 1) * keep_two
    conv_sum = taps[2] * gated + taps[1] * prev_one + taps[0] * prev_two
    mixed = (out_gate * conv_sum).astype(BF)
    mixed = mixed.reshape(count, part)
    mixed, row_pieces = lax.optimization_barrier((mixed, row_pieces))
    conv_out_rows, attn_output_rows = place(row_pieces, owned)
    hidden_one = residual + scatter_plane(dot(mixed, conv_out_rows, 1, 0))

    whole_one, packed_two = lax.optimization_barrier((whole_one, packed_two))
    both_two = gather_z(packed_two)

    normed, inverse_one = rms_forward(hidden_one, ffn1_gain)
    normed_one = gather_plane(normed.astype(BF))
    normed_one, qkv_weight = lax.optimization_barrier((normed_one, qkv_weight))
    whole_one = whole_one.reshape(planes, 3 * unit, width)
    both_one = whole_one[:, : 2 * unit].reshape(-1, width)
    down_one = whole_one[:, 2 * unit :].reshape(-1, width)
    gate_one, up_one, act_one = ffn_up(normed_one, both_one, planes)
    hidden_two = hidden_one + scatter_plane(dot(act_one, down_one, 0, 0))

    normed, inverse_attn = rms_forward(hidden_two, attn_gain)
    normed_attn = gather_plane(normed.astype(BF))
    normed_attn, cotangent_low = lax.optimization_barrier((normed_attn, cotangent))
    cotangent_all = gather_plane(cotangent_low)
    raw_qkv = dot(qkv_weight, normed_attn, 0, 1)
    query_raw = raw_qkv[: heads * head].reshape(heads, head, count)
    key_raw = raw_qkv[heads * head : (heads + 1) * head][None]
    value_low = raw_qkv[(heads + 1) * head :].astype(BF)
    gains = qk_gains.astype(F32)
    query_gain, key_gain = gains[0][None, :, None], gains[1][None, :, None]
    half = head // 2
    frequency = jnp.power(
        jnp.float32(ROPE_BASE), -jnp.arange(half, dtype=F32) * 2.0 / head
    )
    angles = frequency[:, None] * positions.astype(F32)[None, :]
    cosine, sine = jnp.cos(angles)[None], jnp.sin(angles)[None]

    def rope(v):
        first, second = v[:, :half], v[:, half:]
        return jnp.concatenate(
            [first * cosine - second * sine, second * cosine + first * sine], 1
        )

    def rope_back(g):
        first, second = g[:, :half], g[:, half:]
        return jnp.concatenate(
            [first * cosine + second * sine, second * cosine - first * sine], 1
        )

    query_unit, query_inverse = rms_forward(query_raw, query_gain, 1)
    key_unit, key_inverse = rms_forward(key_raw, key_gain, 1)
    query_low = rope(query_unit).astype(BF)
    key_low = rope(key_unit).astype(BF)[0]

    tiles = count // TILE

    query_rows = (query_low.astype(F32) * (head**-0.5)).astype(BF).reshape(heads * head, count)
    row_info = jnp.stack([positions, starts])
    tile_first = (own // 2 ^ jnp.arange(tiles, dtype=jnp.int32)) * TILE
    core = own % 2 * rows
    tile_starts = jnp.max(
        jnp.where(
            doc_starts[None, :]
            <= (z * count + tile_first[:, None, None] + jnp.array([[0], [TILE - 1]])),
            doc_starts[None, None, :],
            0,
        ),
        2,
    )

    def meta_of(step):
        return jnp.concatenate(
            [
                jnp.stack([(z >= step).astype(jnp.int32), core]),
                (z - step) * count + tile_first,
                z * count + tile_first,
                tile_starts[:, 0],
                tile_starts[:, 1],
            ]
        ).astype(jnp.int32)

    metas = [meta_of(step) for step in range(planes)]
    pair = jnp.concatenate([key_low, value_low], 0)
    pair, both_two = lax.optimization_barrier((pair, both_two))
    pairs = [pair] + [from_below(pair, step) for step in range(1, planes)]
    pairs[-1], ffn2_down = lax.optimization_barrier((pairs[-1], ffn2_down))
    down_two = gather_z(ffn2_down)
    acc = jnp.zeros((heads * head, count), F32)
    total = jnp.zeros((heads, count), F32)
    for step in range(planes):
        acc, total = attend(metas[step], pairs[step], query_rows, row_info, acc, total)
    log_total = jnp.log2(total)
    mixed_heads = acc.reshape(heads, head, count) / total[:, None, :]
    head_low = mixed_heads.astype(BF).reshape(heads * head, count)
    hidden_three = hidden_two + scatter_plane(dot(head_low, attn_output_rows, 0, 0))

    normed, inverse_two = rms_forward(hidden_three, ffn2_gain)
    normed_two = gather_plane(normed.astype(BF))
    act_grad_two = dot(down_two, cotangent_all, 1, 1)
    gate_two, up_two, act_two = ffn_up(normed_two, both_two, planes)
    hidden_grad, partial = ffn_back(act_grad_two, gate_two, up_two, normed_two, both_two)
    normed_grad = scatter_plane(partial)
    down_two_terms = by_plane(dot(act_two, cotangent_all, 1, 0), planes)
    both_two_terms = by_plane(dot(hidden_grad, normed_two, 1, 0), planes)
    normed_grad, both_two_terms, down_two_terms = lax.optimization_barrier(
        (normed_grad, both_two_terms, down_two_terms)
    )
    down_two_sum = scatter_z(down_two_terms)
    residual_grad, gain_rows_two = rms_backward(hidden_three, inverse_two, ffn2_gain, normed_grad)
    gradient = cotangent.astype(F32) + residual_grad
    gradient_low = gather_plane(gradient.astype(BF))
    out_grad = dot(attn_output_rows, gradient_low, 1, 1).astype(BF)
    delta = jnp.sum(out_grad.astype(F32).reshape(mixed_heads.shape) * mixed_heads, 1)
    attn_output_terms = by_plane(dot(head_low, gradient_low, 1, 0), planes)

    query_grad = jnp.zeros((heads * head, count), F32)
    arrived = []
    for step in range(planes - 1, -1, -1):
        if len(arrived) > 1:
            query_grad, arrived[-2] = lax.optimization_barrier((query_grad, arrived[-2]))
        query_grad, pair_grad = attend_back(
            metas[step],
            pairs[step],
            query_rows,
            out_grad,
            row_info,
            log_total,
            delta,
            query_grad,
            BF if step > 0 else F32,
        )
        if step > 0:
            arrived.append(from_above(pair_grad, step))
    for block in arrived:
        pair_grad = pair_grad + block.astype(F32)
    pair_grad, both_two_terms, down_two_sum, attn_output_terms = lax.optimization_barrier(
        (pair_grad, both_two_terms, down_two_sum, attn_output_terms)
    )
    both_two_sum = scatter_z(both_two_terms)
    query_tok = query_grad.reshape(heads, head, count) * (head**-0.5)
    query_raw_grad, query_gain_rows = rms_backward(
        query_raw, query_inverse, query_gain, rope_back(query_tok), 1
    )
    key_raw_grad, key_gain_rows = rms_backward(
        key_raw, key_inverse, key_gain, rope_back(pair_grad[None, :head]), 1
    )
    qk_rows = jnp.stack(
        [jnp.sum(query_gain_rows, (0, 2)), jnp.sum(key_gain_rows, (0, 2))]
    ).reshape(-1)
    qkv_grad = jnp.concatenate(
        [
            query_raw_grad.reshape(heads * head, count).astype(BF),
            key_raw_grad[0].astype(BF),
            pair_grad[head:].astype(BF),
        ],
        0,
    )
    normed_grad = scatter_plane(dot(qkv_grad, qkv_weight, 0, 1))
    residual_grad, gain_rows_attn = rms_backward(hidden_two, inverse_attn, attn_gain, normed_grad)
    gradient = gradient + residual_grad
    qkv_weight_grad = dot(normed_attn, qkv_grad, 0, 1)

    qkv_blocks = swap_all(qkv_weight_grad.astype(BF).reshape(devices, owned, -1))

    gradient_low = gather_plane(gradient.astype(BF))
    gradient_low, both_two_sum, qkv_blocks = lax.optimization_barrier(
        (gradient_low, both_two_sum, qkv_blocks)
    )
    down_one_terms = by_plane(dot(act_one, gradient_low, 1, 0), planes)
    act_grad_one = dot(down_one, gradient_low, 1, 1)
    hidden_grad, partial = ffn_back(act_grad_one, gate_one, up_one, normed_one, both_one)
    partial, down_one_terms = lax.optimization_barrier((partial, down_one_terms))
    normed_grad = scatter_plane(partial)
    both_one_terms = by_plane(dot(hidden_grad, normed_one, 1, 0), planes)
    terms_one = jnp.concatenate([both_one_terms, down_one_terms], 1)
    normed_grad, terms_one = lax.optimization_barrier((normed_grad, terms_one))
    sum_one = scatter_z(terms_one)
    grad_ffn2 = ffn_shards(both_two_sum, down_two_sum)
    residual_grad, gain_rows_one = rms_backward(hidden_one, inverse_one, ffn1_gain, normed_grad)
    gradient = gradient + residual_grad

    gradient_low = gather_plane(gradient.astype(BF))
    mixed_grad = dot(gradient_low, conv_out_rows, 1, 1).reshape(8, rows, part)
    row_terms = jnp.concatenate(
        [by_plane(dot(mixed, gradient_low, 0, 0), planes), attn_output_terms], 1
    )
    out_gate_grad = mixed_grad * conv_sum
    conv_grad = mixed_grad * out_gate
    kernel_grad = jnp.stack(
        [
            jnp.sum(conv_grad * prev_two, (0, 1)),
            jnp.sum(conv_grad * prev_one, (0, 1)),
            jnp.sum(conv_grad * gated, (0, 1)),
        ],
        1,
    )
    back_one = taps[1] * conv_grad * keep_one
    back_two = taps[0] * conv_grad * keep_two
    fronts = jnp.concatenate([back_one[:, :1], back_two[:, :2]], 1)
    rim = lax.ppermute(
        pick(fronts, jnp.full((1,), 0)), "z", [(i + 1, i) for i in range(planes - 1)]
    )
    after = pick(fronts, places + 1) + jnp.where(places == 7, 1.0, 0.0)[:, None, None] * rim
    gated_grad = (
        taps[2] * conv_grad
        + jnp.concatenate([back_one[:, 1:], after[:, :1]], 1)
        + jnp.concatenate([back_two[:, 2:], after[:, 1:]], 1)
    )
    projected_grad = (
        jnp.concatenate([gated_grad * conv_values, out_gate_grad, gated_grad * in_gate], 2)
        .astype(BF)
        .reshape(count, 3 * part)
    )
    act_two, projected_grad = lax.optimization_barrier((act_two, projected_grad))
    partial = dot(projected_grad, conv_weight, 1, 1)
    gain_conv = jnp.sum(partial * (raw * raw_inverse), 0)
    partial, row_terms = lax.optimization_barrier((partial, row_terms))
    conv_in_terms = dot(normed_conv, projected_grad, 0, 0).astype(BF)
    out_parts = dot(act_two, down_two, 0, 0).astype(BF)

    kernel_all = lax.dynamic_update_slice(jnp.zeros((width, 3), F32), kernel_grad, (own * part, 0))
    small_grads = jnp.concatenate(
        [
            gain_conv.reshape(devices, owned),
            jnp.sum(gain_rows_one, 0).reshape(devices, owned),
            jnp.sum(gain_rows_attn, 0).reshape(devices, owned),
            jnp.sum(gain_rows_two, 0).reshape(devices, owned),
            kernel_all.reshape(devices, 3 * owned),
            jnp.broadcast_to(qk_rows[None], (devices, qk_rows.shape[0])),
        ],
        1,
    )
    normed_grad, (out_parts, small_grads) = scatter_plane(partial, out_parts, small_grads)
    small_grads = lax.all_to_all(
        small_grads[:, None, :], EVERY, split_axis=0, concat_axis=0, tiled=True
    )
    output_sum = scatter_plane(out_parts)
    normed_grad, sum_one, conv_in_terms, small_grads, row_terms = lax.optimization_barrier(
        (normed_grad, sum_one, conv_in_terms, small_grads, row_terms)
    )
    grad_ffn1 = ffn_shards(sum_one[: 2 * unit], sum_one[2 * unit :])
    row_sum = scatter_z(row_terms)
    output = (hidden_three + output_sum).astype(BF)
    blocks = swap_all(conv_in_terms.reshape(devices, owned, -1))
    row_sum, blocks = lax.optimization_barrier((row_sum, blocks))
    row_sum = row_block_to_owner(row_sum).astype(F32)
    grad_conv_out, grad_attn_output = row_sum[:owned], row_sum[owned:]
    query_part = heads * head
    grad_query, grad_key, grad_value = lanes_back(
        qkv_blocks,
        (8 * query_part, 8 * head, 8 * head),
        lambda j, outs: (
            (0, query_part, outs[0], j * query_part),
            (query_part, head, outs[1], j * head),
            (query_part + head, head, outs[2], j * head),
        ),
    )
    (grad_conv_in,) = lanes_back(
        blocks,
        (3 * width,),
        lambda j, outs: tuple(
            (i * part, part, outs[0], (i * 8 + j) * part) for i in range(3)
        ),
    )
    inverse = lax.rsqrt(jnp.mean(residual * residual, axis=-1, keepdims=True) + EPSILON)
    residual_grad, _ = rms_backward(residual, inverse, conv_gain, normed_grad)
    grad_tokens = gradient + residual_grad
    small_grads = jnp.sum(small_grads, (0, 1))
    grad_norms = [small_grads[i * owned : (i + 1) * owned] for i in range(4)]
    grad_kernel = small_grads[4 * owned : 7 * owned].reshape(owned, 3)
    grad_gains = small_grads[7 * owned :].reshape(2, head)

    return (
        output,
        grad_tokens,
        grad_norms[0],
        grad_conv_in,
        grad_kernel,
        grad_conv_out,
        grad_norms[1],
        grad_ffn1[0],
        grad_ffn1[1],
        grad_ffn1[2],
        grad_norms[2],
        grad_query,
        grad_key,
        grad_value,
        grad_gains,
        grad_attn_output,
        grad_norms[3],
        grad_ffn2[0],
        grad_ffn2[1],
        grad_ffn2[2],
    )


def solution(mesh):
    seq, heads = mesh.shape["seq"], mesh.shape["head"]
    grid = Mesh(mesh.devices.reshape(seq // 2, 2, heads // 2, 2), EVERY)
    lead, both, last = P(EVERY), P(EVERY, None), P(None, EVERY)
    return jax.shard_map(
        body,
        mesh=grid,
        in_specs=(
            both,
            P(),
            lead,
            both,
            both,
            both,
            lead,
            last,
            last,
            both,
            lead,
            both,
            both,
            both,
            P(),
            both,
            lead,
            last,
            last,
            both,
            both,
        ),
        out_specs=(
            both,
            both,
            lead,
            both,
            both,
            both,
            lead,
            last,
            last,
            both,
            lead,
            both,
            both,
            both,
            P(),
            both,
            lead,
            last,
            last,
            both,
        ),
        check_vma=False,
    )
```

```python
import functools

import jax
import jax.numpy as jnp
from jax import lax
from jax.experimental import pallas as pl
from jax.experimental.pallas import tpu as pltpu
from jax.sharding import Mesh
from jax.sharding import PartitionSpec as P

EPSILON = 1e-05
ROPE_BASE = 1000000.0
LOG2E = 1.4426950408889634
BF = jnp.bfloat16
F32 = jnp.float32
PLANE = ("x", "y", "c")
EVERY = ("z", "x", "y", "c")
TILE = 256


def dot(left, right, left_dim, right_dim):
    return lax.dot_general(
        left, right, (((left_dim,), (right_dim,)), ((), ())), preferred_element_type=F32
    )


def rms_forward(values, gain, axis=-1):
    inverse = lax.rsqrt(jnp.mean(values * values, axis=axis, keepdims=True) + EPSILON)
    return values * inverse * gain, inverse


def rms_backward(values, inverse, gain, gradient, axis=-1):
    unit = values * inverse
    scaled = gradient * gain
    result = inverse * (scaled - unit * jnp.mean(scaled * unit, axis=axis, keepdims=True))
    return result, gradient * unit


def plane_index():
    return lax.axis_index(PLANE)


def swap_all(blocks):
    return lax.all_to_all(blocks, EVERY, split_axis=0, concat_axis=0, tiled=True)


SWAP = [(0, 1), (1, 0)]


def core_swap(block):
    return lax.ppermute(block, "c", SWAP)


def chip_swap(block, distance):
    return lax.ppermute(block, ("x", "y"), [(i, i ^ distance) for i in range(4)])


def join_kernel(take, *refs):
    pieces, outs = refs[: -len(take)], refs[-len(take) :]
    first = 0
    for rows, out in zip(take, outs):
        for i, piece in enumerate(pieces):
            out[i * rows : (i + 1) * rows, :] = piece[first : first + rows, :]
        first += rows


def join(pieces, take=None):
    rows, width = pieces[0].shape
    take = take or (rows,)
    vmem = pl.BlockSpec(memory_space=pltpu.VMEM)
    out = pl.pallas_call(
        functools.partial(join_kernel, take),
        out_shape=tuple(
            jax.ShapeDtypeStruct((len(pieces) * t, width), pieces[0].dtype) for t in take
        ),
        in_specs=[vmem] * len(pieces),
        out_specs=(vmem,) * len(take),
        compiler_params=pltpu.CompilerParams(vmem_limit_bytes=16 * 1024 * 1024),
        cost_estimate=pl.CostEstimate(
            flops=0, bytes_accessed=4 * len(pieces) * rows * width, transcendentals=0
        ),
    )(*pieces)
    return out if len(take) > 1 else out[0]


def pack_kernel(*refs):
    gate, up, out = refs[0], refs[1], refs[-1]
    unit = gate.shape[1]
    out[:unit, :] = gate[...].astype(F32).T.astype(BF)
    out[unit : 2 * unit, :] = up[...].astype(F32).T.astype(BF)
    if len(refs) > 3:
        out[2 * unit :, :] = refs[2][...]


def pack(gate, up, *down):
    width, unit = gate.shape
    if unit % 16:
        return jnp.concatenate([gate.T, up.T, *down], 0)
    vmem = pl.BlockSpec(memory_space=pltpu.VMEM)
    rows = (2 + len(down)) * unit
    return pl.pallas_call(
        pack_kernel,
        out_shape=jax.ShapeDtypeStruct((rows, width), BF),
        in_specs=[vmem] * (2 + len(down)),
        out_specs=vmem,
        compiler_params=pltpu.CompilerParams(vmem_limit_bytes=16 * 1024 * 1024),
        cost_estimate=pl.CostEstimate(flops=0, bytes_accessed=4 * rows * width, transcendentals=0),
    )(gate, up, *down)


def unpack_kernel(both, gate, up):
    unit = both.shape[0] // 2
    gate[...] = both[:unit, :].astype(F32).T
    up[...] = both[unit:, :].astype(F32).T


def unpack(both):
    unit, width = both.shape[0] // 2, both.shape[1]
    if unit % 16:
        both = both.astype(F32)
        return both[:unit].T, both[unit:].T
    vmem = pl.BlockSpec(memory_space=pltpu.VMEM)
    out = jax.ShapeDtypeStruct((width, unit), F32)
    return pl.pallas_call(
        unpack_kernel,
        out_shape=(out, out),
        in_specs=[vmem],
        out_specs=(vmem, vmem),
        compiler_params=pltpu.CompilerParams(vmem_limit_bytes=16 * 1024 * 1024),
        cost_estimate=pl.CostEstimate(
            flops=0, bytes_accessed=12 * unit * width, transcendentals=0
        ),
    )(both)


def lanes_kernel(splits, blocks, *outs):
    planes = blocks.shape[0] // 8
    for j in range(8):
        block = blocks[j].astype(F32)
        for k in range(1, planes):
            block = block + blocks[8 * k + j].astype(F32)
        for first, size, out, place in splits(j, outs):
            out[:, place : place + size] = block[:, first : first + size]


def lanes_back(blocks, widths, splits):
    vmem = pl.BlockSpec(memory_space=pltpu.VMEM)
    rows = blocks.shape[1]
    return pl.pallas_call(
        functools.partial(lanes_kernel, splits),
        out_shape=tuple(jax.ShapeDtypeStruct((rows, w), F32) for w in widths),
        in_specs=[vmem],
        out_specs=(vmem,) * len(widths),
        compiler_params=pltpu.CompilerParams(vmem_limit_bytes=16 * 1024 * 1024),
        cost_estimate=pl.CostEstimate(
            flops=0, bytes_accessed=4 * blocks.size, transcendentals=0
        ),
    )(blocks)


def spread_kernel(weight, small, out):
    part = weight.shape[1] // 24
    for j in range(8):
        for i in range(3):
            first = (i * 8 + j) * part
            out[j, :, i * part : (i + 1) * part] = weight[:, first : first + part]
        out[j, :, 3 * part :] = small[...]
    for k in range(8, out.shape[0]):
        out[k] = out[k % 8]


def spread(weight, small, devices):
    rows = weight.shape[0]
    width = weight.shape[1] // 8 + small.shape[1]
    if rows % 16:
        columns = jnp.concatenate(
            [
                weight.reshape(rows, 3, 8, -1).transpose(2, 0, 1, 3).reshape(8, rows, -1),
                jnp.broadcast_to(small[None], (8,) + small.shape),
            ],
            2,
        )
        return jnp.tile(columns, (devices // 8, 1, 1))
    vmem = pl.BlockSpec(memory_space=pltpu.VMEM)
    return pl.pallas_call(
        spread_kernel,
        out_shape=jax.ShapeDtypeStruct((devices, rows, width), BF),
        in_specs=[vmem] * 2,
        out_specs=vmem,
        compiler_params=pltpu.CompilerParams(vmem_limit_bytes=16 * 1024 * 1024),
        cost_estimate=pl.CostEstimate(
            flops=0, bytes_accessed=4 * devices * rows * width, transcendentals=0
        ),
    )(weight, small)


def gather_plane(piece):
    return gather_cores([piece] + [chip_swap(piece, d) for d in (1, 2, 3)])


def gather_cores(chips, take=None):
    return join([v for chip in chips for v in (chip, core_swap(chip))], take)


def place_kernel(cut, z, *refs):
    planes = len(refs) - 2
    pieces, first, second = refs[:planes], refs[-2], refs[-1]
    rest = pieces[0].shape[0] - cut
    for t, piece in enumerate(pieces):
        k = (z[0] - t + planes) % planes
        first[pl.ds(pl.multiple_of(k * cut, cut), cut), :] = piece[:cut, :]
        second[pl.ds(pl.multiple_of(k * rest, rest), rest), :] = piece[cut:, :]


def place(pieces, cut):
    planes = len(pieces)
    rows, width = pieces[0].shape
    z = lax.axis_index("z")
    if cut % 16 or rows % 16:
        stack = jnp.stack(pieces)
        order = [
            lax.dynamic_index_in_dim(stack, (z - k) % planes, 0, keepdims=False)
            for k in range(planes)
        ]
        return (
            jnp.concatenate([v[:cut] for v in order], 0),
            jnp.concatenate([v[cut:] for v in order], 0),
        )
    vmem = pl.BlockSpec(memory_space=pltpu.VMEM)
    return pl.pallas_call(
        functools.partial(place_kernel, cut),
        out_shape=(
            jax.ShapeDtypeStruct((planes * cut, width), BF),
            jax.ShapeDtypeStruct((planes * (rows - cut), width), BF),
        ),
        in_specs=[pl.BlockSpec(memory_space=pltpu.SMEM)] + [vmem] * planes,
        out_specs=(vmem, vmem),
        compiler_params=pltpu.CompilerParams(vmem_limit_bytes=16 * 1024 * 1024),
        cost_estimate=pl.CostEstimate(
            flops=0, bytes_accessed=4 * planes * rows * width, transcendentals=0
        ),
    )(z.reshape(1).astype(jnp.int32), *pieces)


def scatter_plane(parts, *later):
    low = parts.astype(BF).reshape(4, 2, parts.shape[0] // 8, parts.shape[1])
    other = core_swap(low[:, 1])
    mine = [low[d, 0].astype(F32) + other[d].astype(F32) for d in range(4)]
    sent = tuple(mine[d].astype(BF) for d in (3, 1, 2))
    if later:
        sent, later = lax.optimization_barrier((sent, later))
    total = mine[0]
    for d, block in zip((3, 1, 2), sent):
        total = total + chip_swap(block, d).astype(F32)
    return (total, later) if later else total


def rows_of_plane_index(first, second):
    planes = lax.axis_size("z")
    piece = jnp.concatenate([first, second], 0)
    got = []
    for t in range(planes):
        pairs = [
            (j * planes + k, (k + t) % planes * 8 + j) for j in range(8) for k in range(planes)
        ]
        got.append(lax.ppermute(piece, EVERY, pairs))
    return got


def row_block_to_owner(block):
    planes = lax.axis_size("z")
    pairs = [(i * 8 + j, j * planes + i) for j in range(8) for i in range(planes)]
    return lax.ppermute(block, EVERY, pairs)


def from_below(block, distance):
    planes = lax.axis_size("z")
    return lax.ppermute(block, "z", [(i, i + distance) for i in range(planes - distance)])


def from_above(block, distance):
    planes = lax.axis_size("z")
    return lax.ppermute(block, "z", [(i + distance, i) for i in range(planes - distance)])


def gather_z(piece):
    return lax.all_gather(piece, "z", axis=0, tiled=True)


def scatter_z(terms):
    return lax.psum_scatter(terms.astype(BF), "z", scatter_dimension=0, tiled=False)


def tile_masks(meta, key_tile, query_tile):
    key_first = meta[2 + key_tile]
    key_last = key_first + (TILE - 1)
    query_first = meta[6 + query_tile]
    query_last = query_first + (TILE - 1)
    start_first = meta[10 + query_tile]
    start_last = meta[14 + query_tile]
    some = (key_last >= start_first) & (key_first <= query_last)
    whole = (key_first >= start_last) & (key_last <= query_first)
    return some, whole


def key_positions(meta, key_tile, count, width):
    row = lax.broadcasted_iota(jnp.int32, (TILE, width), 0) ^ meta[1]
    parts = [meta[2 + key_tile + i] + row for i in range(count)]
    return jnp.concatenate(parts, 0) if count > 1 else parts[0]


def visit_tiles(meta, tiles, work):
    def query_step(q, _):
        needed, whole = jnp.int32(0), jnp.int32(0)
        for k in range(tiles):
            some, all_ = tile_masks(meta, k, q)
            needed += some.astype(jnp.int32)
            whole += all_.astype(jnp.int32)
        strip = needed >= tiles - 1
        pl.when(whole == tiles)(lambda: work(q, 0, tiles, False))
        pl.when(strip & (whole < tiles))(lambda: work(q, 0, tiles, True))

        @pl.when(jnp.logical_not(strip) & (needed > 0))
        def _():
            def key_step(k, _):
                some, all_ = tile_masks(meta, k, q)
                pl.when(some & all_)(lambda: work(q, k, 1, False))
                pl.when(some & jnp.logical_not(all_))(lambda: work(q, k, 1, True))
                return 0

            lax.fori_loop(0, tiles, key_step, 0)

        return 0

    lax.fori_loop(0, tiles, query_step, 0)


def beside(ref, parts, rows, columns):
    return jnp.concatenate([ref[i * rows : (i + 1) * rows, columns] for i in range(parts)], 1)


def forward_kernel(meta, pair, query, rows, acc_in, total_in, acc, total, keys):
    head = pair.shape[0] // 2
    heads = query.shape[0] // head
    tiles = pair.shape[1] // TILE
    acc[...] = acc_in[...]
    total[...] = total_in[...]

    @pl.when(meta[0] > 0)
    def _():
        keys[...] = pair[:head, :].astype(F32).T.astype(BF)

        def work(q, k, count, masked):
            columns = pl.ds(pl.multiple_of(q * TILE, TILE), TILE)
            span = pl.ds(pl.multiple_of(k * TILE, TILE), count * TILE)
            scores = dot(keys[span, :], beside(query, heads, head, columns), 1, 0)
            terms = jnp.exp2(scores * LOG2E)
            if masked:
                key_pos = key_positions(meta, k, count, terms.shape[1])
                last = jnp.concatenate([rows[0:1, columns]] * heads, 1)
                first = jnp.concatenate([rows[1:2, columns]] * heads, 1)
                terms = jnp.where((key_pos <= last) & (key_pos >= first), terms, 0.0)
            sums = jnp.sum(terms, 0, keepdims=True)
            values = dot(pair[head:, span], terms.astype(BF), 1, 0)
            for h in range(heads):
                here = slice(h * TILE, (h + 1) * TILE)
                total[h : h + 1, columns] += sums[:, here]
                acc[h * head : (h + 1) * head, columns] += values[:, here]

        visit_tiles(meta, tiles, work)


def attend(meta, pair, query, rows, acc, total):
    head = pair.shape[0] // 2
    count = pair.shape[1]
    vmem = pl.BlockSpec(memory_space=pltpu.VMEM)
    return pl.pallas_call(
        forward_kernel,
        out_shape=(
            jax.ShapeDtypeStruct(acc.shape, F32),
            jax.ShapeDtypeStruct(total.shape, F32),
        ),
        in_specs=[pl.BlockSpec(memory_space=pltpu.SMEM)] + [vmem] * 5,
        out_specs=(vmem, vmem),
        scratch_shapes=[pltpu.VMEM((count, head), BF)],
        compiler_params=pltpu.CompilerParams(vmem_limit_bytes=32 * 1024 * 1024),
        cost_estimate=pl.CostEstimate(flops=0, bytes_accessed=pair.size, transcendentals=0),
    )(meta, pair, query, rows, acc, total)


def backward_kernel(
    meta,
    pair,
    query,
    out_grad,
    rows,
    log_total,
    delta,
    query_in,
    query_grad,
    pair_out,
    keys,
    values,
    pair_grad,
):
    head = pair.shape[0] // 2
    heads = query.shape[0] // head
    tiles = pair.shape[1] // TILE
    query_grad[...] = query_in[...]
    pair_grad[...] = jnp.zeros(pair_grad.shape, F32)

    @pl.when(meta[0] > 0)
    def _():
        keys[...] = pair[:head, :].astype(F32).T.astype(BF)
        values[...] = pair[head:, :].astype(F32).T.astype(BF)

        def work(q, k, count, masked):
            columns = pl.ds(pl.multiple_of(q * TILE, TILE), TILE)
            span = pl.ds(pl.multiple_of(k * TILE, TILE), count * TILE)
            queries = beside(query, heads, head, columns)
            outs = beside(out_grad, heads, head, columns)
            scores = dot(keys[span, :], queries, 1, 0)
            weights = jnp.exp2(scores * LOG2E - beside(log_total, heads, 1, columns))
            if masked:
                key_pos = key_positions(meta, k, count, weights.shape[1])
                last = jnp.concatenate([rows[0:1, columns]] * heads, 1)
                first = jnp.concatenate([rows[1:2, columns]] * heads, 1)
                weights = jnp.where((key_pos <= last) & (key_pos >= first), weights, 0.0)
            weight_grad = dot(values[span, :], outs, 1, 0)
            score_grad = (weights * (weight_grad - beside(delta, heads, 1, columns))).astype(BF)
            pair_grad[:head, span] += dot(queries, score_grad, 1, 1)
            pair_grad[head:, span] += dot(outs, weights.astype(BF), 1, 1)
            more = dot(pair[:head, span], score_grad, 1, 0)
            for h in range(heads):
                query_grad[h * head : (h + 1) * head, columns] += more[
                    :, h * TILE : (h + 1) * TILE
                ]

        visit_tiles(meta, tiles, work)

    pair_out[...] = pair_grad[...].astype(pair_out.dtype)


def attend_back(meta, pair, query, out_grad, rows, log_total, delta, query_grad, dtype):
    head = pair.shape[0] // 2
    count = pair.shape[1]
    vmem = pl.BlockSpec(memory_space=pltpu.VMEM)
    return pl.pallas_call(
        backward_kernel,
        out_shape=(
            jax.ShapeDtypeStruct(query_grad.shape, F32),
            jax.ShapeDtypeStruct(pair.shape, dtype),
        ),
        in_specs=[pl.BlockSpec(memory_space=pltpu.SMEM)] + [vmem] * 7,
        out_specs=(vmem, vmem),
        scratch_shapes=[
            pltpu.VMEM((count, head), BF),
            pltpu.VMEM((count, head), BF),
            pltpu.VMEM(pair.shape, F32),
        ],
        compiler_params=pltpu.CompilerParams(vmem_limit_bytes=32 * 1024 * 1024),
        cost_estimate=pl.CostEstimate(
            flops=0, bytes_accessed=pair.size, transcendentals=0
        ),
    )(meta, pair, query, out_grad, rows, log_total, delta, query_grad)


def ffn_up(normed, both, planes):
    hidden = dot(both, normed, 1, 1)
    hidden = hidden.reshape(planes, 2, -1, hidden.shape[-1])
    gate, up = hidden[:, 0], hidden[:, 1]
    act = (jax.nn.silu(gate) * up).astype(BF)
    return gate, up, act.reshape(-1, act.shape[-1])


def ffn_back(act_grad, gate, up, normed, both):
    act_grad = act_grad.reshape(gate.shape)
    sig = jax.nn.sigmoid(gate)
    gate_grad = (act_grad * up * sig * (1.0 + gate * (1.0 - sig))).astype(BF)
    up_grad = (act_grad * gate * sig).astype(BF)
    hidden_grad = jnp.stack([gate_grad, up_grad], 1).reshape(-1, gate.shape[-1])
    return hidden_grad, dot(hidden_grad, both, 0, 0)


def by_plane(grad, planes):
    return grad.astype(BF).reshape(planes, -1, grad.shape[-1])


def ffn_shards(both, down):
    return unpack(both) + (down.astype(F32),)


def body(
    tokens,
    doc_starts,
    conv_norm,
    conv_in,
    conv_kernel,
    conv_out,
    ffn1_norm,
    ffn1_gate,
    ffn1_up_weight,
    ffn1_down,
    attn_norm,
    attn_query,
    attn_key,
    attn_value,
    qk_gains,
    attn_output,
    ffn2_norm,
    ffn2_gate,
    ffn2_up_weight,
    ffn2_down,
    cotangent,
):
    planes = lax.axis_size("z")
    z = lax.axis_index("z")
    own = plane_index()
    rows, width = tokens.shape
    count = 8 * rows
    owned = conv_norm.shape[0]
    head = qk_gains.shape[1]
    heads = attn_query.shape[1] // (8 * head)
    part = width // 8
    devices = 8 * planes

    places = own ^ jnp.arange(8, dtype=jnp.int32)
    positions = z * count + places[:, None] * rows + jnp.arange(rows, dtype=jnp.int32)[None, :]
    positions = positions.reshape(-1)
    starts = jnp.max(
        jnp.where(doc_starts[None, :] <= positions[:, None], doc_starts[None, :], 0), 1
    )
    keep_one = (positions - 1 >= starts).astype(F32).reshape(8, rows, 1)
    keep_two = (positions - 2 >= starts).astype(F32).reshape(8, rows, 1)

    small = jnp.stack([conv_norm, ffn1_norm, attn_norm, ffn2_norm], 1)
    small = jnp.concatenate([small, conv_kernel, jnp.zeros((owned, 121), BF)], 1)
    columns = spread(conv_in, small, devices)
    columns, tokens = lax.optimization_barrier((columns, tokens))
    columns = swap_all(columns).reshape(width, -1)
    unit = ffn1_down.shape[0]
    query_columns = jnp.concatenate(
        [
            attn_query.reshape(owned, 8, -1).transpose(1, 0, 2),
            attn_key.reshape(owned, 8, -1).transpose(1, 0, 2),
            attn_value.reshape(owned, 8, -1).transpose(1, 0, 2),
        ],
        2,
    )
    columns, query_columns = lax.optimization_barrier((columns, query_columns))
    qkv_weight = swap_all(jnp.tile(query_columns, (planes, 1, 1))).reshape(width, -1)
    packed_two = pack(ffn2_gate, ffn2_up_weight)
    conv_weight = columns[:, : 3 * part]
    small = columns[:, 3 * part : 3 * part + 8].T.astype(F32)
    conv_gain, ffn1_gain, attn_gain, ffn2_gain = (small[i : i + 1] for i in range(4))
    taps = lax.dynamic_slice(small[4:7], (0, own * part), (3, part))[:, None, None, :]

    edge = from_below(tokens[rows - 16 :], 1)
    piece = jnp.concatenate([tokens, edge], 0)
    chips = [piece] + [chip_swap(piece, d) for d in (1, 2, 3)]
    chips[1], ffn1_gate = lax.optimization_barrier((chips[1], ffn1_gate))
    packed_one = pack(ffn1_gate, ffn1_up_weight, ffn1_down)
    chips[1], packed_one, conv_out = lax.optimization_barrier((chips[1], packed_one, conv_out))
    tokens_all, edges = gather_cores(chips, (rows, 16))
    below = lax.dynamic_slice(edges, ((own ^ 7) * 16, 0), (16, width)).astype(F32)
    whole_one = gather_z(packed_one)
    row_pieces = rows_of_plane_index(conv_out, attn_output)
    raw = tokens_all.astype(F32)

    residual = tokens.astype(F32)
    normed_conv, raw_inverse = rms_forward(raw, conv_gain)
    normed_conv = normed_conv.astype(BF)
    projected = dot(normed_conv, conv_weight, 1, 0).reshape(8, rows, 3 * part)
    in_gate = projected[..., :part]
    out_gate = projected[..., part : 2 * part]
    conv_values = projected[..., 2 * part :]
    gated = in_gate * conv_values
    def pick(table, wanted):
        chosen = (places[None, :] == wanted[:, None]).astype(F32)
        return jnp.sum(chosen[:, :, None, None] * table[None], 1)

    tails = gated[:, rows - 2 :]
    normed_below, _ = rms_forward(below, conv_gain)
    rim = dot(normed_below.astype(BF), conv_weight, 1, 0)[14:]
    rim = (rim[:, :part] * rim[:, 2 * part :])[None]
    before = pick(tails, places - 1) + jnp.where(places == 0, 1.0, 0.0)[:, None, None] * rim
    prev_one = jnp.concatenate([before[:, 1:], gated[:, :-1]], 1) * keep_one
    prev_two = jnp.concatenate([before, gated[:, :-2]], 1) * keep_two
    conv_sum = taps[2] * gated + taps[1] * prev_one + taps[0] * prev_two
    mixed = (out_gate * conv_sum).astype(BF)
    mixed = mixed.reshape(count, part)
    mixed, row_pieces = lax.optimization_barrier((mixed, row_pieces))
    conv_out_rows, attn_output_rows = place(row_pieces, owned)
    hidden_one = residual + scatter_plane(dot(mixed, conv_out_rows, 1, 0))

    whole_one, packed_two = lax.optimization_barrier((whole_one, packed_two))
    both_two = gather_z(packed_two)

    normed, inverse_one = rms_forward(hidden_one, ffn1_gain)
    normed_one = gather_plane(normed.astype(BF))
    normed_one, qkv_weight = lax.optimization_barrier((normed_one, qkv_weight))
    whole_one = whole_one.reshape(planes, 3 * unit, width)
    both_one = whole_one[:, : 2 * unit].reshape(-1, width)
    down_one = whole_one[:, 2 * unit :].reshape(-1, width)
    gate_one, up_one, act_one = ffn_up(normed_one, both_one, planes)
    hidden_two = hidden_one + scatter_plane(dot(act_one, down_one, 0, 0))

    normed, inverse_attn = rms_forward(hidden_two, attn_gain)
    normed_attn = gather_plane(normed.astype(BF))
    normed_attn, cotangent_low = lax.optimization_barrier((normed_attn, cotangent))
    cotangent_all = gather_plane(cotangent_low)
    raw_qkv = dot(qkv_weight, normed_attn, 0, 1)
    query_raw = raw_qkv[: heads * head].reshape(heads, head, count)
    key_raw = raw_qkv[heads * head : (heads + 1) * head][None]
    value_low = raw_qkv[(heads + 1) * head :].astype(BF)
    gains = qk_gains.astype(F32)
    query_gain, key_gain = gains[0][None, :, None], gains[1][None, :, None]
    half = head // 2
    frequency = jnp.power(
        jnp.float32(ROPE_BASE), -jnp.arange(half, dtype=F32) * 2.0 / head
    )
    angles = frequency[:, None] * positions.astype(F32)[None, :]
    cosine, sine = jnp.cos(angles)[None], jnp.sin(angles)[None]

    def rope(v):
        first, second = v[:, :half], v[:, half:]
        return jnp.concatenate(
            [first * cosine - second * sine, second * cosine + first * sine], 1
        )

    def rope_back(g):
        first, second = g[:, :half], g[:, half:]
        return jnp.concatenate(
            [first * cosine + second * sine, second * cosine - first * sine], 1
        )

    query_unit, query_inverse = rms_forward(query_raw, query_gain, 1)
    key_unit, key_inverse = rms_forward(key_raw, key_gain, 1)
    query_low = rope(query_unit).astype(BF)
    key_low = rope(key_unit).astype(BF)[0]

    tiles = count // TILE

    query_rows = (query_low.astype(F32) * (head**-0.5)).astype(BF).reshape(heads * head, count)
    row_info = jnp.stack([positions, starts])
    tile_first = (own // 2 ^ jnp.arange(tiles, dtype=jnp.int32)) * TILE
    core = own % 2 * rows
    tile_starts = jnp.max(
        jnp.where(
            doc_starts[None, :]
            <= (z * count + tile_first[:, None, None] + jnp.array([[0], [TILE - 1]])),
            doc_starts[None, None, :],
            0,
        ),
        2,
    )

    def meta_of(step):
        return jnp.concatenate(
            [
                jnp.stack([(z >= step).astype(jnp.int32), core]),
                (z - step) * count + tile_first,
                z * count + tile_first,
                tile_starts[:, 0],
                tile_starts[:, 1],
            ]
        ).astype(jnp.int32)

    metas = [meta_of(step) for step in range(planes)]
    pair = jnp.concatenate([key_low, value_low], 0)
    pair, both_two = lax.optimization_barrier((pair, both_two))
    pairs = [pair] + [from_below(pair, step) for step in range(1, planes)]
    pairs[-1], ffn2_down = lax.optimization_barrier((pairs[-1], ffn2_down))
    down_two = gather_z(ffn2_down)
    acc = jnp.zeros((heads * head, count), F32)
    total = jnp.zeros((heads, count), F32)
    for step in range(planes):
        acc, total = attend(metas[step], pairs[step], query_rows, row_info, acc, total)
    log_total = jnp.log2(total)
    mixed_heads = acc.reshape(heads, head, count) / total[:, None, :]
    head_low = mixed_heads.astype(BF).reshape(heads * head, count)
    hidden_three = hidden_two + scatter_plane(dot(head_low, attn_output_rows, 0, 0))

    normed, inverse_two = rms_forward(hidden_three, ffn2_gain)
    normed_two = gather_plane(normed.astype(BF))
    act_grad_two = dot(down_two, cotangent_all, 1, 1)
    gate_two, up_two, act_two = ffn_up(normed_two, both_two, planes)
    hidden_grad, partial = ffn_back(act_grad_two, gate_two, up_two, normed_two, both_two)
    normed_grad = scatter_plane(partial)
    down_two_terms = by_plane(dot(act_two, cotangent_all, 1, 0), planes)
    both_two_terms = by_plane(dot(hidden_grad, normed_two, 1, 0), planes)
    normed_grad, both_two_terms, down_two_terms = lax.optimization_barrier(
        (normed_grad, both_two_terms, down_two_terms)
    )
    down_two_sum = scatter_z(down_two_terms)
    residual_grad, gain_rows_two = rms_backward(hidden_three, inverse_two, ffn2_gain, normed_grad)
    gradient = cotangent.astype(F32) + residual_grad
    gradient_low = gather_plane(gradient.astype(BF))
    out_grad = dot(attn_output_rows, gradient_low, 1, 1).astype(BF)
    delta = jnp.sum(out_grad.astype(F32).reshape(mixed_heads.shape) * mixed_heads, 1)
    attn_output_terms = by_plane(dot(head_low, gradient_low, 1, 0), planes)

    query_grad = jnp.zeros((heads * head, count), F32)
    arrived = []
    for step in range(planes - 1, -1, -1):
        if len(arrived) > 1 or step == 0:
            late = -1 if step == 0 else -2
            query_grad, arrived[late] = lax.optimization_barrier((query_grad, arrived[late]))
        query_grad, pair_grad = attend_back(
            metas[step],
            pairs[step],
            query_rows,
            out_grad,
            row_info,
            log_total,
            delta,
            query_grad,
            BF if step > 0 else F32,
        )
        if step > 0:
            arrived.append(from_above(pair_grad, step))
    for block in arrived:
        pair_grad = pair_grad + block.astype(F32)
    pair_grad, both_two_terms, down_two_sum, attn_output_terms = lax.optimization_barrier(
        (pair_grad, both_two_terms, down_two_sum, attn_output_terms)
    )
    both_two_sum = scatter_z(both_two_terms)
    query_tok = query_grad.reshape(heads, head, count) * (head**-0.5)
    query_raw_grad, query_gain_rows = rms_backward(
        query_raw, query_inverse, query_gain, rope_back(query_tok), 1
    )
    key_raw_grad, key_gain_rows = rms_backward(
        key_raw, key_inverse, key_gain, rope_back(pair_grad[None, :head]), 1
    )
    qk_rows = jnp.stack(
        [jnp.sum(query_gain_rows, (0, 2)), jnp.sum(key_gain_rows, (0, 2))]
    ).reshape(-1)
    qkv_grad = jnp.concatenate(
        [
            query_raw_grad.reshape(heads * head, count).astype(BF),
            key_raw_grad[0].astype(BF),
            pair_grad[head:].astype(BF),
        ],
        0,
    )
    normed_grad = scatter_plane(dot(qkv_grad, qkv_weight, 0, 1))
    residual_grad, gain_rows_attn = rms_backward(hidden_two, inverse_attn, attn_gain, normed_grad)
    gradient = gradient + residual_grad
    qkv_weight_grad = dot(normed_attn, qkv_grad, 0, 1)

    qkv_blocks = swap_all(qkv_weight_grad.astype(BF).reshape(devices, owned, -1))

    gradient_low = gather_plane(gradient.astype(BF))
    gradient_low, both_two_sum, qkv_blocks = lax.optimization_barrier(
        (gradient_low, both_two_sum, qkv_blocks)
    )
    down_one_terms = by_plane(dot(act_one, gradient_low, 1, 0), planes)
    act_grad_one = dot(down_one, gradient_low, 1, 1)
    hidden_grad, partial = ffn_back(act_grad_one, gate_one, up_one, normed_one, both_one)
    partial, down_one_terms = lax.optimization_barrier((partial, down_one_terms))
    normed_grad = scatter_plane(partial)
    both_one_terms = by_plane(dot(hidden_grad, normed_one, 1, 0), planes)
    terms_one = jnp.concatenate([both_one_terms, down_one_terms], 1)
    normed_grad, terms_one = lax.optimization_barrier((normed_grad, terms_one))
    sum_one = scatter_z(terms_one)
    grad_ffn2 = ffn_shards(both_two_sum, down_two_sum)
    residual_grad, gain_rows_one = rms_backward(hidden_one, inverse_one, ffn1_gain, normed_grad)
    gradient = gradient + residual_grad

    gradient_low = gather_plane(gradient.astype(BF))
    mixed_grad = dot(gradient_low, conv_out_rows, 1, 1).reshape(8, rows, part)
    row_terms = jnp.concatenate(
        [by_plane(dot(mixed, gradient_low, 0, 0), planes), attn_output_terms], 1
    )
    out_gate_grad = mixed_grad * conv_sum
    conv_grad = mixed_grad * out_gate
    kernel_grad = jnp.stack(
        [
            jnp.sum(conv_grad * prev_two, (0, 1)),
            jnp.sum(conv_grad * prev_one, (0, 1)),
            jnp.sum(conv_grad * gated, (0, 1)),
        ],
        1,
    )
    back_one = taps[1] * conv_grad * keep_one
    back_two = taps[0] * conv_grad * keep_two
    fronts = jnp.concatenate([back_one[:, :1], back_two[:, :2]], 1)
    rim = lax.ppermute(
        pick(fronts, jnp.full((1,), 0)), "z", [(i + 1, i) for i in range(planes - 1)]
    )
    after = pick(fronts, places + 1) + jnp.where(places == 7, 1.0, 0.0)[:, None, None] * rim
    gated_grad = (
        taps[2] * conv_grad
        + jnp.concatenate([back_one[:, 1:], after[:, :1]], 1)
        + jnp.concatenate([back_two[:, 2:], after[:, 1:]], 1)
    )
    projected_grad = (
        jnp.concatenate([gated_grad * conv_values, out_gate_grad, gated_grad * in_gate], 2)
        .astype(BF)
        .reshape(count, 3 * part)
    )
    act_two, projected_grad = lax.optimization_barrier((act_two, projected_grad))
    partial = dot(projected_grad, conv_weight, 1, 1)
    gain_conv = jnp.sum(partial * (raw * raw_inverse), 0)
    partial, row_terms = lax.optimization_barrier((partial, row_terms))
    conv_in_terms = dot(normed_conv, projected_grad, 0, 0).astype(BF)
    out_parts = dot(act_two, down_two, 0, 0).astype(BF)

    kernel_all = lax.dynamic_update_slice(jnp.zeros((width, 3), F32), kernel_grad, (own * part, 0))
    small_grads = jnp.concatenate(
        [
            gain_conv.reshape(devices, owned),
            jnp.sum(gain_rows_one, 0).reshape(devices, owned),
            jnp.sum(gain_rows_attn, 0).reshape(devices, owned),
            jnp.sum(gain_rows_two, 0).reshape(devices, owned),
            kernel_all.reshape(devices, 3 * owned),
            jnp.broadcast_to(qk_rows[None], (devices, qk_rows.shape[0])),
        ],
        1,
    )
    normed_grad, (out_parts, small_grads) = scatter_plane(partial, out_parts, small_grads)
    small_grads = lax.all_to_all(
        small_grads[:, None, :], EVERY, split_axis=0, concat_axis=0, tiled=True
    )
    normed_grad, sum_one, conv_in_terms, small_grads, row_terms = lax.optimization_barrier(
        (normed_grad, sum_one, conv_in_terms, small_grads, row_terms)
    )
    grad_ffn1 = ffn_shards(sum_one[: 2 * unit], sum_one[2 * unit :])
    output_sum = scatter_plane(out_parts)
    row_sum = lax.all_to_all(row_terms, "z", split_axis=0, concat_axis=0, tiled=True)
    row_sum = jnp.sum(row_sum.astype(F32), 0).astype(BF)
    output = (hidden_three + output_sum).astype(BF)
    blocks = swap_all(conv_in_terms.reshape(devices, owned, -1))
    row_sum = row_block_to_owner(row_sum).astype(F32)
    grad_conv_out, grad_attn_output = row_sum[:owned], row_sum[owned:]
    query_part = heads * head
    grad_query, grad_key, grad_value = lanes_back(
        qkv_blocks,
        (8 * query_part, 8 * head, 8 * head),
        lambda j, outs: (
            (0, query_part, outs[0], j * query_part),
            (query_part, head, outs[1], j * head),
            (query_part + head, head, outs[2], j * head),
        ),
    )
    (grad_conv_in,) = lanes_back(
        blocks,
        (3 * width,),
        lambda j, outs: tuple(
            (i * part, part, outs[0], (i * 8 + j) * part) for i in range(3)
        ),
    )
    inverse = lax.rsqrt(jnp.mean(residual * residual, axis=-1, keepdims=True) + EPSILON)
    residual_grad, _ = rms_backward(residual, inverse, conv_gain, normed_grad)
    grad_tokens = gradient + residual_grad
    small_grads = jnp.sum(small_grads, (0, 1))
    grad_norms = [small_grads[i * owned : (i + 1) * owned] for i in range(4)]
    grad_kernel = small_grads[4 * owned : 7 * owned].reshape(owned, 3)
    grad_gains = small_grads[7 * owned :].reshape(2, head)

    return (
        output,
        grad_tokens,
        grad_norms[0],
        grad_conv_in,
        grad_kernel,
        grad_conv_out,
        grad_norms[1],
        grad_ffn1[0],
        grad_ffn1[1],
        grad_ffn1[2],
        grad_norms[2],
        grad_query,
        grad_key,
        grad_value,
        grad_gains,
        grad_attn_output,
        grad_norms[3],
        grad_ffn2[0],
        grad_ffn2[1],
        grad_ffn2[2],
    )


def solution(mesh):
    seq, heads = mesh.shape["seq"], mesh.shape["head"]
    grid = Mesh(mesh.devices.reshape(seq // 2, 2, heads // 2, 2), EVERY)
    lead, both, last = P(EVERY), P(EVERY, None), P(None, EVERY)
    return jax.shard_map(
        body,
        mesh=grid,
        in_specs=(
            both,
            P(),
            lead,
            both,
            both,
            both,
            lead,
            last,
            last,
            both,
            lead,
            both,
            both,
            both,
            P(),
            both,
            lead,
            last,
            last,
            both,
            both,
        ),
        out_specs=(
            both,
            both,
            lead,
            both,
            both,
            both,
            lead,
            last,
            last,
            both,
            lead,
            both,
            both,
            both,
            P(),
            both,
            lead,
            last,
            last,
            both,
        ),
        check_vma=False,
    )
```

```python
import functools

import jax
import jax.numpy as jnp
from jax import lax
from jax.experimental import pallas as pl
from jax.experimental.pallas import tpu as pltpu
from jax.sharding import Mesh
from jax.sharding import PartitionSpec as P

EPSILON = 1e-05
ROPE_BASE = 1000000.0
LOG2E = 1.4426950408889634
BF = jnp.bfloat16
F32 = jnp.float32
PLANE = ("x", "y", "c")
EVERY = ("z", "x", "y", "c")
TILE = 256


def dot(left, right, left_dim, right_dim):
    return lax.dot_general(
        left, right, (((left_dim,), (right_dim,)), ((), ())), preferred_element_type=F32
    )


def rms_forward(values, gain, axis=-1):
    inverse = lax.rsqrt(jnp.mean(values * values, axis=axis, keepdims=True) + EPSILON)
    return values * inverse * gain, inverse


def rms_backward(values, inverse, gain, gradient, axis=-1):
    unit = values * inverse
    scaled = gradient * gain
    result = inverse * (scaled - unit * jnp.mean(scaled * unit, axis=axis, keepdims=True))
    return result, gradient * unit


def plane_index():
    return lax.axis_index(PLANE)


def swap_all(blocks):
    return lax.all_to_all(blocks, EVERY, split_axis=0, concat_axis=0, tiled=True)


SWAP = [(0, 1), (1, 0)]


def core_swap(block):
    return lax.ppermute(block, "c", SWAP)


def chip_swap(block, distance):
    return lax.ppermute(block, ("x", "y"), [(i, i ^ distance) for i in range(4)])


def join_kernel(take, *refs):
    done = refs[-1]
    pieces, outs = refs[: -len(take) - 1], refs[-len(take) - 1 : -1]
    copies = []
    for i, piece in enumerate(pieces):
        first = 0
        for t, (rows, out) in enumerate(zip(take, outs)):
            copies.append(
                pltpu.make_async_copy(
                    piece.at[first : first + rows, :],
                    out.at[i * rows : (i + 1) * rows, :],
                    done.at[i * len(take) + t],
                )
            )
            first += rows
    for copy in copies:
        copy.start()
    for copy in copies:
        copy.wait()


def join(pieces, take=None):
    rows, width = pieces[0].shape
    take = take or (rows,)
    out = pl.pallas_call(
        functools.partial(join_kernel, take),
        out_shape=tuple(
            jax.ShapeDtypeStruct((len(pieces) * t, width), pieces[0].dtype) for t in take
        ),
        in_specs=[pl.BlockSpec(memory_space=pl.ANY)] * len(pieces),
        out_specs=(pl.BlockSpec(memory_space=pltpu.VMEM),) * len(take),
        scratch_shapes=[pltpu.SemaphoreType.DMA((len(pieces) * len(take),))],
        compiler_params=pltpu.CompilerParams(vmem_limit_bytes=16 * 1024 * 1024),
        cost_estimate=pl.CostEstimate(
            flops=0, bytes_accessed=4 * len(pieces) * rows * width, transcendentals=0
        ),
    )(*pieces)
    return out if len(take) > 1 else out[0]


def pack(gate, up, *down):
    pieces = [gate.T, up.T, *down]
    if gate.shape[1] % 16:
        return jnp.concatenate(pieces, 0)
    return join(pieces)


def unpack_kernel(both, gate, up):
    unit = both.shape[0] // 2
    gate[...] = both[:unit, :].astype(F32).T
    up[...] = both[unit:, :].astype(F32).T


def unpack(both):
    unit, width = both.shape[0] // 2, both.shape[1]
    if unit % 16:
        both = both.astype(F32)
        return both[:unit].T, both[unit:].T
    vmem = pl.BlockSpec(memory_space=pltpu.VMEM)
    out = jax.ShapeDtypeStruct((width, unit), F32)
    return pl.pallas_call(
        unpack_kernel,
        out_shape=(out, out),
        in_specs=[vmem],
        out_specs=(vmem, vmem),
        compiler_params=pltpu.CompilerParams(vmem_limit_bytes=16 * 1024 * 1024),
        cost_estimate=pl.CostEstimate(
            flops=0, bytes_accessed=12 * unit * width, transcendentals=0
        ),
    )(both)


def lanes_kernel(splits, blocks, *outs):
    planes = blocks.shape[0] // 8
    for j in range(8):
        block = blocks[j].astype(F32)
        for k in range(1, planes):
            block = block + blocks[8 * k + j].astype(F32)
        for first, size, out, place in splits(j, outs):
            out[:, place : place + size] = block[:, first : first + size]


def lanes_back(blocks, widths, splits):
    vmem = pl.BlockSpec(memory_space=pltpu.VMEM)
    rows = blocks.shape[1]
    return pl.pallas_call(
        functools.partial(lanes_kernel, splits),
        out_shape=tuple(jax.ShapeDtypeStruct((rows, w), F32) for w in widths),
        in_specs=[vmem],
        out_specs=(vmem,) * len(widths),
        compiler_params=pltpu.CompilerParams(vmem_limit_bytes=16 * 1024 * 1024),
        cost_estimate=pl.CostEstimate(
            flops=0, bytes_accessed=4 * blocks.size, transcendentals=0
        ),
    )(blocks)


def spread_kernel(weight, small, out):
    part = weight.shape[1] // 24
    for j in range(8):
        for i in range(3):
            first = (i * 8 + j) * part
            out[j, :, i * part : (i + 1) * part] = weight[:, first : first + part]
        out[j, :, 3 * part :] = small[...]
    for k in range(8, out.shape[0]):
        out[k] = out[k % 8]


def spread(weight, small, devices):
    rows = weight.shape[0]
    width = weight.shape[1] // 8 + small.shape[1]
    if rows % 16:
        columns = jnp.concatenate(
            [
                weight.reshape(rows, 3, 8, -1).transpose(2, 0, 1, 3).reshape(8, rows, -1),
                jnp.broadcast_to(small[None], (8,) + small.shape),
            ],
            2,
        )
        return jnp.tile(columns, (devices // 8, 1, 1))
    vmem = pl.BlockSpec(memory_space=pltpu.VMEM)
    return pl.pallas_call(
        spread_kernel,
        out_shape=jax.ShapeDtypeStruct((devices, rows, width), BF),
        in_specs=[vmem] * 2,
        out_specs=vmem,
        compiler_params=pltpu.CompilerParams(vmem_limit_bytes=16 * 1024 * 1024),
        cost_estimate=pl.CostEstimate(
            flops=0, bytes_accessed=4 * devices * rows * width, transcendentals=0
        ),
    )(weight, small)


def gather_plane(piece):
    return gather_cores([piece] + [chip_swap(piece, d) for d in (1, 2, 3)])


def gather_cores(chips, take=None):
    return join([v for chip in chips for v in (chip, core_swap(chip))], take)


def place_kernel(cut, z, *refs):
    planes = len(refs) - 2
    pieces, first, second = refs[:planes], refs[-2], refs[-1]
    rest = pieces[0].shape[0] - cut
    for t, piece in enumerate(pieces):
        k = (z[0] - t + planes) % planes
        first[pl.ds(pl.multiple_of(k * cut, cut), cut), :] = piece[:cut, :]
        second[pl.ds(pl.multiple_of(k * rest, rest), rest), :] = piece[cut:, :]


def place(pieces, cut):
    planes = len(pieces)
    rows, width = pieces[0].shape
    z = lax.axis_index("z")
    if cut % 16 or rows % 16:
        stack = jnp.stack(pieces)
        order = [
            lax.dynamic_index_in_dim(stack, (z - k) % planes, 0, keepdims=False)
            for k in range(planes)
        ]
        return (
            jnp.concatenate([v[:cut] for v in order], 0),
            jnp.concatenate([v[cut:] for v in order], 0),
        )
    vmem = pl.BlockSpec(memory_space=pltpu.VMEM)
    return pl.pallas_call(
        functools.partial(place_kernel, cut),
        out_shape=(
            jax.ShapeDtypeStruct((planes * cut, width), BF),
            jax.ShapeDtypeStruct((planes * (rows - cut), width), BF),
        ),
        in_specs=[pl.BlockSpec(memory_space=pltpu.SMEM)] + [vmem] * planes,
        out_specs=(vmem, vmem),
        compiler_params=pltpu.CompilerParams(vmem_limit_bytes=16 * 1024 * 1024),
        cost_estimate=pl.CostEstimate(
            flops=0, bytes_accessed=4 * planes * rows * width, transcendentals=0
        ),
    )(z.reshape(1).astype(jnp.int32), *pieces)


def scatter_plane(parts, *later):
    low = parts.astype(BF).reshape(4, 2, parts.shape[0] // 8, parts.shape[1])
    other = core_swap(low[:, 1])
    mine = [low[d, 0].astype(F32) + other[d].astype(F32) for d in range(4)]
    sent = tuple(mine[d].astype(BF) for d in (3, 1, 2))
    if later:
        sent, later = lax.optimization_barrier((sent, later))
    total = mine[0]
    for d, block in zip((3, 1, 2), sent):
        total = total + chip_swap(block, d).astype(F32)
    return (total, later) if later else total


def rows_of_plane_index(first, second):
    planes = lax.axis_size("z")
    piece = jnp.concatenate([first, second], 0)
    got = []
    for t in range(planes):
        pairs = [
            (j * planes + k, (k + t) % planes * 8 + j) for j in range(8) for k in range(planes)
        ]
        got.append(lax.ppermute(piece, EVERY, pairs))
    return got


def row_block_to_owner(block):
    planes = lax.axis_size("z")
    pairs = [(i * 8 + j, j * planes + i) for j in range(8) for i in range(planes)]
    return lax.ppermute(block, EVERY, pairs)


def from_below(block, distance):
    planes = lax.axis_size("z")
    return lax.ppermute(block, "z", [(i, i + distance) for i in range(planes - distance)])


def from_above(block, distance):
    planes = lax.axis_size("z")
    return lax.ppermute(block, "z", [(i + distance, i) for i in range(planes - distance)])


def gather_z(piece):
    return lax.all_gather(piece, "z", axis=0, tiled=True)


def scatter_z(terms):
    return lax.psum_scatter(terms.astype(BF), "z", scatter_dimension=0, tiled=False)


def tile_masks(meta, key_tile, query_tile):
    key_first = meta[2 + key_tile]
    key_last = key_first + (TILE - 1)
    query_first = meta[6 + query_tile]
    query_last = query_first + (TILE - 1)
    start_first = meta[10 + query_tile]
    start_last = meta[14 + query_tile]
    some = (key_last >= start_first) & (key_first <= query_last)
    whole = (key_first >= start_last) & (key_last <= query_first)
    return some, whole


def key_positions(meta, key_tile, count, width):
    row = lax.broadcasted_iota(jnp.int32, (TILE, width), 0) ^ meta[1]
    parts = [meta[2 + key_tile + i] + row for i in range(count)]
    return jnp.concatenate(parts, 0) if count > 1 else parts[0]


def visit_tiles(meta, tiles, work):
    def query_step(q, _):
        needed, whole = jnp.int32(0), jnp.int32(0)
        for k in range(tiles):
            some, all_ = tile_masks(meta, k, q)
            needed += some.astype(jnp.int32)
            whole += all_.astype(jnp.int32)
        strip = needed >= tiles - 1
        pl.when(whole == tiles)(lambda: work(q, 0, tiles, False))
        pl.when(strip & (whole < tiles))(lambda: work(q, 0, tiles, True))

        @pl.when(jnp.logical_not(strip) & (needed > 0))
        def _():
            def key_step(k, _):
                some, all_ = tile_masks(meta, k, q)
                pl.when(some & all_)(lambda: work(q, k, 1, False))
                pl.when(some & jnp.logical_not(all_))(lambda: work(q, k, 1, True))
                return 0

            lax.fori_loop(0, tiles, key_step, 0)

        return 0

    lax.fori_loop(0, tiles, query_step, 0)


def beside(ref, parts, rows, columns):
    return jnp.concatenate([ref[i * rows : (i + 1) * rows, columns] for i in range(parts)], 1)


def forward_kernel(meta, pair, query, rows, acc_in, total_in, acc, total, keys):
    head = pair.shape[0] // 2
    heads = query.shape[0] // head
    tiles = pair.shape[1] // TILE
    acc[...] = acc_in[...]
    total[...] = total_in[...]

    @pl.when(meta[0] > 0)
    def _():
        keys[...] = pair[:head, :].astype(F32).T.astype(BF)

        def work(q, k, count, masked):
            columns = pl.ds(pl.multiple_of(q * TILE, TILE), TILE)
            span = pl.ds(pl.multiple_of(k * TILE, TILE), count * TILE)
            scores = dot(keys[span, :], beside(query, heads, head, columns), 1, 0)
            terms = jnp.exp2(scores * LOG2E)
            if masked:
                key_pos = key_positions(meta, k, count, terms.shape[1])
                last = jnp.concatenate([rows[0:1, columns]] * heads, 1)
                first = jnp.concatenate([rows[1:2, columns]] * heads, 1)
                terms = jnp.where((key_pos <= last) & (key_pos >= first), terms, 0.0)
            sums = jnp.sum(terms, 0, keepdims=True)
            values = dot(pair[head:, span], terms.astype(BF), 1, 0)
            for h in range(heads):
                here = slice(h * TILE, (h + 1) * TILE)
                total[h : h + 1, columns] += sums[:, here]
                acc[h * head : (h + 1) * head, columns] += values[:, here]

        visit_tiles(meta, tiles, work)


def attend(meta, pair, query, rows, acc, total):
    head = pair.shape[0] // 2
    count = pair.shape[1]
    vmem = pl.BlockSpec(memory_space=pltpu.VMEM)
    return pl.pallas_call(
        forward_kernel,
        out_shape=(
            jax.ShapeDtypeStruct(acc.shape, F32),
            jax.ShapeDtypeStruct(total.shape, F32),
        ),
        in_specs=[pl.BlockSpec(memory_space=pltpu.SMEM)] + [vmem] * 5,
        out_specs=(vmem, vmem),
        scratch_shapes=[pltpu.VMEM((count, head), BF)],
        compiler_params=pltpu.CompilerParams(vmem_limit_bytes=32 * 1024 * 1024),
        cost_estimate=pl.CostEstimate(flops=0, bytes_accessed=pair.size, transcendentals=0),
    )(meta, pair, query, rows, acc, total)


def backward_kernel(
    meta,
    pair,
    query,
    out_grad,
    rows,
    log_total,
    delta,
    query_in,
    query_grad,
    pair_out,
    keys,
    values,
    pair_grad,
):
    head = pair.shape[0] // 2
    heads = query.shape[0] // head
    tiles = pair.shape[1] // TILE
    query_grad[...] = query_in[...]
    pair_grad[...] = jnp.zeros(pair_grad.shape, F32)

    @pl.when(meta[0] > 0)
    def _():
        keys[...] = pair[:head, :].astype(F32).T.astype(BF)
        values[...] = pair[head:, :].astype(F32).T.astype(BF)

        def work(q, k, count, masked):
            columns = pl.ds(pl.multiple_of(q * TILE, TILE), TILE)
            span = pl.ds(pl.multiple_of(k * TILE, TILE), count * TILE)
            queries = beside(query, heads, head, columns)
            outs = beside(out_grad, heads, head, columns)
            scores = dot(keys[span, :], queries, 1, 0)
            weights = jnp.exp2(scores * LOG2E - beside(log_total, heads, 1, columns))
            if masked:
                key_pos = key_positions(meta, k, count, weights.shape[1])
                last = jnp.concatenate([rows[0:1, columns]] * heads, 1)
                first = jnp.concatenate([rows[1:2, columns]] * heads, 1)
                weights = jnp.where((key_pos <= last) & (key_pos >= first), weights, 0.0)
            weight_grad = dot(values[span, :], outs, 1, 0)
            score_grad = (weights * (weight_grad - beside(delta, heads, 1, columns))).astype(BF)
            pair_grad[:head, span] += dot(queries, score_grad, 1, 1)
            pair_grad[head:, span] += dot(outs, weights.astype(BF), 1, 1)
            more = dot(pair[:head, span], score_grad, 1, 0)
            for h in range(heads):
                query_grad[h * head : (h + 1) * head, columns] += more[
                    :, h * TILE : (h + 1) * TILE
                ]

        visit_tiles(meta, tiles, work)

    pair_out[...] = pair_grad[...].astype(pair_out.dtype)


def attend_back(meta, pair, query, out_grad, rows, log_total, delta, query_grad, dtype):
    head = pair.shape[0] // 2
    count = pair.shape[1]
    vmem = pl.BlockSpec(memory_space=pltpu.VMEM)
    return pl.pallas_call(
        backward_kernel,
        out_shape=(
            jax.ShapeDtypeStruct(query_grad.shape, F32),
            jax.ShapeDtypeStruct(pair.shape, dtype),
        ),
        in_specs=[pl.BlockSpec(memory_space=pltpu.SMEM)] + [vmem] * 7,
        out_specs=(vmem, vmem),
        scratch_shapes=[
            pltpu.VMEM((count, head), BF),
            pltpu.VMEM((count, head), BF),
            pltpu.VMEM(pair.shape, F32),
        ],
        compiler_params=pltpu.CompilerParams(vmem_limit_bytes=32 * 1024 * 1024),
        cost_estimate=pl.CostEstimate(
            flops=0, bytes_accessed=pair.size, transcendentals=0
        ),
    )(meta, pair, query, out_grad, rows, log_total, delta, query_grad)


def ffn_up(normed, both, planes):
    hidden = dot(both, normed, 1, 1)
    hidden = hidden.reshape(planes, 2, -1, hidden.shape[-1])
    gate, up = hidden[:, 0], hidden[:, 1]
    act = (jax.nn.silu(gate) * up).astype(BF)
    return gate, up, act.reshape(-1, act.shape[-1])


def ffn_back(act_grad, gate, up, normed, both):
    act_grad = act_grad.reshape(gate.shape)
    sig = jax.nn.sigmoid(gate)
    gate_grad = (act_grad * up * sig * (1.0 + gate * (1.0 - sig))).astype(BF)
    up_grad = (act_grad * gate * sig).astype(BF)
    hidden_grad = jnp.stack([gate_grad, up_grad], 1).reshape(-1, gate.shape[-1])
    return hidden_grad, dot(hidden_grad, both, 0, 0)


def by_plane(grad, planes):
    return grad.astype(BF).reshape(planes, -1, grad.shape[-1])


def ffn_shards(both, down):
    return unpack(both) + (down.astype(F32),)


def body(
    tokens,
    doc_starts,
    conv_norm,
    conv_in,
    conv_kernel,
    conv_out,
    ffn1_norm,
    ffn1_gate,
    ffn1_up_weight,
    ffn1_down,
    attn_norm,
    attn_query,
    attn_key,
    attn_value,
    qk_gains,
    attn_output,
    ffn2_norm,
    ffn2_gate,
    ffn2_up_weight,
    ffn2_down,
    cotangent,
):
    planes = lax.axis_size("z")
    z = lax.axis_index("z")
    own = plane_index()
    rows, width = tokens.shape
    count = 8 * rows
    owned = conv_norm.shape[0]
    head = qk_gains.shape[1]
    heads = attn_query.shape[1] // (8 * head)
    part = width // 8
    devices = 8 * planes

    places = own ^ jnp.arange(8, dtype=jnp.int32)
    positions = z * count + places[:, None] * rows + jnp.arange(rows, dtype=jnp.int32)[None, :]
    positions = positions.reshape(-1)
    starts = jnp.max(
        jnp.where(doc_starts[None, :] <= positions[:, None], doc_starts[None, :], 0), 1
    )
    keep_one = (positions - 1 >= starts).astype(F32).reshape(8, rows, 1)
    keep_two = (positions - 2 >= starts).astype(F32).reshape(8, rows, 1)

    small = jnp.stack([conv_norm, ffn1_norm, attn_norm, ffn2_norm], 1)
    small = jnp.concatenate([small, conv_kernel, jnp.zeros((owned, 121), BF)], 1)
    columns = spread(conv_in, small, devices)
    columns, tokens = lax.optimization_barrier((columns, tokens))
    columns = swap_all(columns).reshape(width, -1)
    unit = ffn1_down.shape[0]
    query_columns = jnp.concatenate(
        [
            attn_query.reshape(owned, 8, -1).transpose(1, 0, 2),
            attn_key.reshape(owned, 8, -1).transpose(1, 0, 2),
            attn_value.reshape(owned, 8, -1).transpose(1, 0, 2),
        ],
        2,
    )
    columns, query_columns = lax.optimization_barrier((columns, query_columns))
    qkv_weight = swap_all(jnp.tile(query_columns, (planes, 1, 1))).reshape(width, -1)
    packed_two = pack(ffn2_gate, ffn2_up_weight)
    conv_weight = columns[:, : 3 * part]
    small = columns[:, 3 * part : 3 * part + 8].T.astype(F32)
    conv_gain, ffn1_gain, attn_gain, ffn2_gain = (small[i : i + 1] for i in range(4))
    taps = lax.dynamic_slice(small[4:7], (0, own * part), (3, part))[:, None, None, :]

    edge = from_below(tokens[rows - 16 :], 1)
    piece = jnp.concatenate([tokens, edge], 0)
    chips = [piece] + [chip_swap(piece, d) for d in (1, 2, 3)]
    chips[1], ffn1_gate = lax.optimization_barrier((chips[1], ffn1_gate))
    packed_one = pack(ffn1_gate, ffn1_up_weight, ffn1_down)
    chips[1], packed_one, conv_out = lax.optimization_barrier((chips[1], packed_one, conv_out))
    tokens_all, edges = gather_cores(chips, (rows, 16))
    below = lax.dynamic_slice(edges, ((own ^ 7) * 16, 0), (16, width)).astype(F32)
    whole_one = gather_z(packed_one)
    row_pieces = rows_of_plane_index(conv_out, attn_output)
    raw = tokens_all.astype(F32)

    residual = tokens.astype(F32)
    normed_conv, raw_inverse = rms_forward(raw, conv_gain)
    normed_conv = normed_conv.astype(BF)
    projected = dot(normed_conv, conv_weight, 1, 0).reshape(8, rows, 3 * part)
    in_gate = projected[..., :part]
    out_gate = projected[..., part : 2 * part]
    conv_values = projected[..., 2 * part :]
    gated = in_gate * conv_values
    def pick(table, wanted):
        chosen = (places[None, :] == wanted[:, None]).astype(F32)
        return jnp.sum(chosen[:, :, None, None] * table[None], 1)

    tails = gated[:, rows - 2 :]
    normed_below, _ = rms_forward(below, conv_gain)
    rim = dot(normed_below.astype(BF), conv_weight, 1, 0)[14:]
    rim = (rim[:, :part] * rim[:, 2 * part :])[None]
    before = pick(tails, places - 1) + jnp.where(places == 0, 1.0, 0.0)[:, None, None] * rim
    prev_one = jnp.concatenate([before[:, 1:], gated[:, :-1]], 1) * keep_one
    prev_two = jnp.concatenate([before, gated[:, :-2]], 1) * keep_two
    conv_sum = taps[2] * gated + taps[1] * prev_one + taps[0] * prev_two
    mixed = (out_gate * conv_sum).astype(BF)
    mixed = mixed.reshape(count, part)
    mixed, row_pieces = lax.optimization_barrier((mixed, row_pieces))
    conv_out_rows, attn_output_rows = place(row_pieces, owned)
    hidden_one = residual + scatter_plane(dot(mixed, conv_out_rows, 1, 0))

    whole_one, packed_two = lax.optimization_barrier((whole_one, packed_two))
    both_two = gather_z(packed_two)

    normed, inverse_one = rms_forward(hidden_one, ffn1_gain)
    normed_one = gather_plane(normed.astype(BF))
    normed_one, qkv_weight = lax.optimization_barrier((normed_one, qkv_weight))
    whole_one = whole_one.reshape(planes, 3 * unit, width)
    both_one = whole_one[:, : 2 * unit].reshape(-1, width)
    down_one = whole_one[:, 2 * unit :].reshape(-1, width)
    gate_one, up_one, act_one = ffn_up(normed_one, both_one, planes)
    hidden_two = hidden_one + scatter_plane(dot(act_one, down_one, 0, 0))

    normed, inverse_attn = rms_forward(hidden_two, attn_gain)
    normed_attn = gather_plane(normed.astype(BF))
    normed_attn, cotangent_low = lax.optimization_barrier((normed_attn, cotangent))
    cotangent_all = gather_plane(cotangent_low)
    raw_qkv = dot(qkv_weight, normed_attn, 0, 1)
    query_raw = raw_qkv[: heads * head].reshape(heads, head, count)
    key_raw = raw_qkv[heads * head : (heads + 1) * head][None]
    value_low = raw_qkv[(heads + 1) * head :].astype(BF)
    gains = qk_gains.astype(F32)
    query_gain, key_gain = gains[0][None, :, None], gains[1][None, :, None]
    half = head // 2
    frequency = jnp.power(
        jnp.float32(ROPE_BASE), -jnp.arange(half, dtype=F32) * 2.0 / head
    )
    angles = frequency[:, None] * positions.astype(F32)[None, :]
    cosine, sine = jnp.cos(angles)[None], jnp.sin(angles)[None]

    def rope(v):
        first, second = v[:, :half], v[:, half:]
        return jnp.concatenate(
            [first * cosine - second * sine, second * cosine + first * sine], 1
        )

    def rope_back(g):
        first, second = g[:, :half], g[:, half:]
        return jnp.concatenate(
            [first * cosine + second * sine, second * cosine - first * sine], 1
        )

    query_unit, query_inverse = rms_forward(query_raw, query_gain, 1)
    key_unit, key_inverse = rms_forward(key_raw, key_gain, 1)
    query_low = rope(query_unit).astype(BF)
    key_low = rope(key_unit).astype(BF)[0]

    tiles = count // TILE

    query_rows = (query_low.astype(F32) * (head**-0.5)).astype(BF).reshape(heads * head, count)
    row_info = jnp.stack([positions, starts])
    tile_first = (own // 2 ^ jnp.arange(tiles, dtype=jnp.int32)) * TILE
    core = own % 2 * rows
    tile_starts = jnp.max(
        jnp.where(
            doc_starts[None, :]
            <= (z * count + tile_first[:, None, None] + jnp.array([[0], [TILE - 1]])),
            doc_starts[None, None, :],
            0,
        ),
        2,
    )

    def meta_of(step):
        return jnp.concatenate(
            [
                jnp.stack([(z >= step).astype(jnp.int32), core]),
                (z - step) * count + tile_first,
                z * count + tile_first,
                tile_starts[:, 0],
                tile_starts[:, 1],
            ]
        ).astype(jnp.int32)

    metas = [meta_of(step) for step in range(planes)]
    pair = jnp.concatenate([key_low, value_low], 0)
    pair, both_two = lax.optimization_barrier((pair, both_two))
    pairs = [pair] + [from_below(pair, step) for step in range(1, planes)]
    pairs[-1], ffn2_down = lax.optimization_barrier((pairs[-1], ffn2_down))
    down_two = gather_z(ffn2_down)
    acc = jnp.zeros((heads * head, count), F32)
    total = jnp.zeros((heads, count), F32)
    for step in range(planes):
        acc, total = attend(metas[step], pairs[step], query_rows, row_info, acc, total)
    log_total = jnp.log2(total)
    mixed_heads = acc.reshape(heads, head, count) / total[:, None, :]
    head_low = mixed_heads.astype(BF).reshape(heads * head, count)
    hidden_three = hidden_two + scatter_plane(dot(head_low, attn_output_rows, 0, 0))

    normed, inverse_two = rms_forward(hidden_three, ffn2_gain)
    normed_two = gather_plane(normed.astype(BF))
    act_grad_two = dot(down_two, cotangent_all, 1, 1)
    gate_two, up_two, act_two = ffn_up(normed_two, both_two, planes)
    hidden_grad, partial = ffn_back(act_grad_two, gate_two, up_two, normed_two, both_two)
    normed_grad = scatter_plane(partial)
    down_two_terms = by_plane(dot(act_two, cotangent_all, 1, 0), planes)
    both_two_terms = by_plane(dot(hidden_grad, normed_two, 1, 0), planes)
    normed_grad, both_two_terms, down_two_terms = lax.optimization_barrier(
        (normed_grad, both_two_terms, down_two_terms)
    )
    down_two_sum = scatter_z(down_two_terms)
    residual_grad, gain_rows_two = rms_backward(hidden_three, inverse_two, ffn2_gain, normed_grad)
    gradient = cotangent.astype(F32) + residual_grad
    gradient_low = gather_plane(gradient.astype(BF))
    out_grad = dot(attn_output_rows, gradient_low, 1, 1).astype(BF)
    delta = jnp.sum(out_grad.astype(F32).reshape(mixed_heads.shape) * mixed_heads, 1)
    attn_output_terms = by_plane(dot(head_low, gradient_low, 1, 0), planes)

    query_grad = jnp.zeros((heads * head, count), F32)
    arrived = []
    for step in range(planes - 1, -1, -1):
        if len(arrived) > 1 or step == 0:
            late = -1 if step == 0 else -2
            query_grad, arrived[late] = lax.optimization_barrier((query_grad, arrived[late]))
        query_grad, pair_grad = attend_back(
            metas[step],
            pairs[step],
            query_rows,
            out_grad,
            row_info,
            log_total,
            delta,
            query_grad,
            BF if step > 0 else F32,
        )
        if step > 0:
            arrived.append(from_above(pair_grad, step))
    for block in arrived:
        pair_grad = pair_grad + block.astype(F32)
    pair_grad, both_two_terms, down_two_sum, attn_output_terms = lax.optimization_barrier(
        (pair_grad, both_two_terms, down_two_sum, attn_output_terms)
    )
    both_two_sum = scatter_z(both_two_terms)
    query_tok = query_grad.reshape(heads, head, count) * (head**-0.5)
    query_raw_grad, query_gain_rows = rms_backward(
        query_raw, query_inverse, query_gain, rope_back(query_tok), 1
    )
    key_raw_grad, key_gain_rows = rms_backward(
        key_raw, key_inverse, key_gain, rope_back(pair_grad[None, :head]), 1
    )
    qk_rows = jnp.stack(
        [jnp.sum(query_gain_rows, (0, 2)), jnp.sum(key_gain_rows, (0, 2))]
    ).reshape(-1)
    qkv_grad = jnp.concatenate(
        [
            query_raw_grad.reshape(heads * head, count).astype(BF),
            key_raw_grad[0].astype(BF),
            pair_grad[head:].astype(BF),
        ],
        0,
    )
    normed_grad = scatter_plane(dot(qkv_grad, qkv_weight, 0, 1))
    residual_grad, gain_rows_attn = rms_backward(hidden_two, inverse_attn, attn_gain, normed_grad)
    gradient = gradient + residual_grad
    qkv_weight_grad = dot(normed_attn, qkv_grad, 0, 1)

    qkv_blocks = swap_all(qkv_weight_grad.astype(BF).reshape(devices, owned, -1))

    gradient_low = gather_plane(gradient.astype(BF))
    gradient_low, both_two_sum, qkv_blocks = lax.optimization_barrier(
        (gradient_low, both_two_sum, qkv_blocks)
    )
    down_one_terms = by_plane(dot(act_one, gradient_low, 1, 0), planes)
    act_grad_one = dot(down_one, gradient_low, 1, 1)
    hidden_grad, partial = ffn_back(act_grad_one, gate_one, up_one, normed_one, both_one)
    partial, down_one_terms = lax.optimization_barrier((partial, down_one_terms))
    normed_grad = scatter_plane(partial)
    both_one_terms = by_plane(dot(hidden_grad, normed_one, 1, 0), planes)
    terms_one = jnp.concatenate([both_one_terms, down_one_terms], 1)
    normed_grad, terms_one = lax.optimization_barrier((normed_grad, terms_one))
    sum_one = scatter_z(terms_one)
    grad_ffn2 = ffn_shards(both_two_sum, down_two_sum)
    residual_grad, gain_rows_one = rms_backward(hidden_one, inverse_one, ffn1_gain, normed_grad)
    gradient = gradient + residual_grad

    gradient_low = gather_plane(gradient.astype(BF))
    mixed_grad = dot(gradient_low, conv_out_rows, 1, 1).reshape(8, rows, part)
    row_terms = jnp.concatenate(
        [by_plane(dot(mixed, gradient_low, 0, 0), planes), attn_output_terms], 1
    )
    out_gate_grad = mixed_grad * conv_sum
    conv_grad = mixed_grad * out_gate
    kernel_grad = jnp.stack(
        [
            jnp.sum(conv_grad * prev_two, (0, 1)),
            jnp.sum(conv_grad * prev_one, (0, 1)),
            jnp.sum(conv_grad * gated, (0, 1)),
        ],
        1,
    )
    back_one = taps[1] * conv_grad * keep_one
    back_two = taps[0] * conv_grad * keep_two
    fronts = jnp.concatenate([back_one[:, :1], back_two[:, :2]], 1)
    rim = lax.ppermute(
        pick(fronts, jnp.full((1,), 0)), "z", [(i + 1, i) for i in range(planes - 1)]
    )
    after = pick(fronts, places + 1) + jnp.where(places == 7, 1.0, 0.0)[:, None, None] * rim
    gated_grad = (
        taps[2] * conv_grad
        + jnp.concatenate([back_one[:, 1:], after[:, :1]], 1)
        + jnp.concatenate([back_two[:, 2:], after[:, 1:]], 1)
    )
    projected_grad = (
        jnp.concatenate([gated_grad * conv_values, out_gate_grad, gated_grad * in_gate], 2)
        .astype(BF)
        .reshape(count, 3 * part)
    )
    act_two, projected_grad = lax.optimization_barrier((act_two, projected_grad))
    partial = dot(projected_grad, conv_weight, 1, 1)
    gain_conv = jnp.sum(partial * (raw * raw_inverse), 0)
    partial, row_terms = lax.optimization_barrier((partial, row_terms))
    conv_in_terms = dot(normed_conv, projected_grad, 0, 0).astype(BF)
    out_parts = dot(act_two, down_two, 0, 0).astype(BF)

    kernel_all = lax.dynamic_update_slice(jnp.zeros((width, 3), F32), kernel_grad, (own * part, 0))
    small_grads = jnp.concatenate(
        [
            gain_conv.reshape(devices, owned),
            jnp.sum(gain_rows_one, 0).reshape(devices, owned),
            jnp.sum(gain_rows_attn, 0).reshape(devices, owned),
            jnp.sum(gain_rows_two, 0).reshape(devices, owned),
            kernel_all.reshape(devices, 3 * owned),
            jnp.broadcast_to(qk_rows[None], (devices, qk_rows.shape[0])),
        ],
        1,
    )
    normed_grad, (out_parts, small_grads) = scatter_plane(partial, out_parts, small_grads)
    small_grads = lax.all_to_all(
        small_grads[:, None, :], EVERY, split_axis=0, concat_axis=0, tiled=True
    )
    normed_grad, sum_one, conv_in_terms, small_grads, row_terms = lax.optimization_barrier(
        (normed_grad, sum_one, conv_in_terms, small_grads, row_terms)
    )
    grad_ffn1 = ffn_shards(sum_one[: 2 * unit], sum_one[2 * unit :])
    output_sum = scatter_plane(out_parts)
    row_sum = lax.all_to_all(row_terms, "z", split_axis=0, concat_axis=0, tiled=True)
    row_sum = jnp.sum(row_sum.astype(F32), 0).astype(BF)
    output = (hidden_three + output_sum).astype(BF)
    blocks = swap_all(conv_in_terms.reshape(devices, owned, -1))
    row_sum = row_block_to_owner(row_sum).astype(F32)
    grad_conv_out, grad_attn_output = row_sum[:owned], row_sum[owned:]
    query_part = heads * head
    grad_query, grad_key, grad_value = lanes_back(
        qkv_blocks,
        (8 * query_part, 8 * head, 8 * head),
        lambda j, outs: (
            (0, query_part, outs[0], j * query_part),
            (query_part, head, outs[1], j * head),
            (query_part + head, head, outs[2], j * head),
        ),
    )
    (grad_conv_in,) = lanes_back(
        blocks,
        (3 * width,),
        lambda j, outs: tuple(
            (i * part, part, outs[0], (i * 8 + j) * part) for i in range(3)
        ),
    )
    inverse = lax.rsqrt(jnp.mean(residual * residual, axis=-1, keepdims=True) + EPSILON)
    residual_grad, _ = rms_backward(residual, inverse, conv_gain, normed_grad)
    grad_tokens = gradient + residual_grad
    small_grads = jnp.sum(small_grads, (0, 1))
    grad_norms = [small_grads[i * owned : (i + 1) * owned] for i in range(4)]
    grad_kernel = small_grads[4 * owned : 7 * owned].reshape(owned, 3)
    grad_gains = small_grads[7 * owned :].reshape(2, head)

    return (
        output,
        grad_tokens,
        grad_norms[0],
        grad_conv_in,
        grad_kernel,
        grad_conv_out,
        grad_norms[1],
        grad_ffn1[0],
        grad_ffn1[1],
        grad_ffn1[2],
        grad_norms[2],
        grad_query,
        grad_key,
        grad_value,
        grad_gains,
        grad_attn_output,
        grad_norms[3],
        grad_ffn2[0],
        grad_ffn2[1],
        grad_ffn2[2],
    )


def solution(mesh):
    seq, heads = mesh.shape["seq"], mesh.shape["head"]
    grid = Mesh(mesh.devices.reshape(seq // 2, 2, heads // 2, 2), EVERY)
    lead, both, last = P(EVERY), P(EVERY, None), P(None, EVERY)
    return jax.shard_map(
        body,
        mesh=grid,
        in_specs=(
            both,
            P(),
            lead,
            both,
            both,
            both,
            lead,
            last,
            last,
            both,
            lead,
            both,
            both,
            both,
            P(),
            both,
            lead,
            last,
            last,
            both,
            both,
        ),
        out_specs=(
            both,
            both,
            lead,
            both,
            both,
            both,
            lead,
            last,
            last,
            both,
            lead,
            both,
            both,
            both,
            P(),
            both,
            lead,
            last,
            last,
            both,
        ),
        check_vma=False,
    )
```
